256 devices in a mesh: space: 32 (over y, z_hi, core), vel: 8 (over x, z_lo).
Axes of the slice: x: 4, y: 4, z: 8 (z_hi: 4, z_lo: 2; z = z_hi * 2 + z_lo), core: 2. Of those that a mesh axis runs over, the one named last changes fastest.
Arguments:
- dist: float32 [13824, 16384], P('vel', 'space'), may hold values from 0.02 to 45, as said below
- free_stream: float32 [13824], P('vel'), may hold values from 0.36 to 14, as said below
- area_normal: float32 [18, 16384], P(None, 'space'), may hold values from -2.7 to 2.7
- cell_volume: float32 [16384], P('space'), may hold values from 0.5 to 2
- face_nbr: int32 [6, 16384], P(None, 'space'), may hold values from 0 to 1023
- face_type: int32 [6, 16384], P(None, 'space'), may hold values from 0 to 2, as said below
- send_list: int32 [4, 4096], P(None, 'space'), may hold values from 0 to 511
Outputs:
- dist_new: float32 [13824, 16384], P('vel', 'space')
The draws below stay inside these ranges and needn't reach their ends.
Inputs may be any that keep to these rules, and one draw needn't show every extreme that they name: `dist`: every entry is positive. `free_stream`: every entry is positive. `face_nbr`: an entry s at or above 512 names received slot s - 512; entries are read only where face_type is 0. `face_type`: 0 interior or partition face, 1 inflow, 2 outflow. `send_list`: local cell numbers of the sending partition.
All inputs are finite; a program needn't handle non-finite values.
Results may differ from the reference program's by a relative error of at most 0.0003.
Values sent between devices are 32-bit elements; how exact they have to be, the bound alone decides.
A program may use at most 128 MiB of HBM per device.

```python
import math
import jax
import jax.numpy as jnp
from jax import lax

NODES = 24
VELS = 13824
CELL_DEV = 512
SEND = 128
DIRS = 4
FACES = 6
CELLS = 16384
N_SPACE = 32


def speed_axes():
    vel_index = jnp.arange(VELS, dtype=jnp.int32)
    half = (NODES - 1) / 2.0
    first = (vel_index // (NODES * NODES)).astype(jnp.float32)
    second = (vel_index // NODES % NODES).astype(jnp.float32)
    last_axis = (vel_index % NODES).astype(jnp.float32)
    return (first - half, second - half, last_axis - half)


def draw_dist(key, part):
    key = jax.random.fold_in(key, 11)
    cell_key, entry_key = jax.random.split(key)
    speed_x, speed_y, speed_z = speed_axes()
    cell_scale = jnp.exp(jax.random.uniform(cell_key, (CELLS,), jnp.float32, -0.7, 0.7))
    noise_part = jax.random.uniform(entry_key, (VELS, CELLS), jnp.float32, -1.0, 1.0)
    return cell_scale[None, :] * jnp.exp(0.1 * speed_x[:, None] + noise_part)


def draw_free_stream(key, part):
    key = jax.random.fold_in(key, 13)
    beam_key, floor_key = jax.random.split(key)
    speed_x, speed_y, speed_z = speed_axes()
    beam = 4.0 * jnp.exp(-((speed_x - 8.0) ** 2 + speed_y ** 2 + speed_z ** 2) / 4.0)
    beam_noise = jax.random.uniform(beam_key, (VELS,), jnp.float32, -1.0, 1.0)
    floor_noise = jax.random.uniform(floor_key, (VELS,), jnp.float32, -1.0, 1.0)
    return beam * jnp.exp(beam_noise) + jnp.exp(floor_noise)


def draw_area_normal(key, part):
    key = jax.random.fold_in(key, 12)
    scale_key, tilt_key = jax.random.split(key)
    face_scale = jnp.exp(jax.random.uniform(scale_key, (FACES, CELLS), jnp.float32, -0.7, 0.7))
    tilt = jax.random.uniform(tilt_key, (FACES, 3, CELLS), jnp.float32, -0.3, 0.3)
    face_ids = jnp.arange(FACES, dtype=jnp.int32)[:, None]
    dim_ids = jnp.arange(3, dtype=jnp.int32)[None, :]
    main_part = jnp.where(dim_ids == face_ids // 2, 1.0 - 2.0 * (face_ids % 2).astype(jnp.float32), 0.0)
    return (face_scale[:, None, :] * (main_part[:, :, None] + tilt)).reshape(3 * FACES, CELLS)


def draw_face_type(key, part):
    key = jax.random.fold_in(key, 14)
    picked = jax.random.randint(key, (FACES, CELLS), 0, 10, dtype=jnp.int32)
    return jnp.where(picked < 7, 0, jnp.where(picked < 9, 1, 2)).astype(jnp.int32)


def place_ends(values, rng, low, top_value):
    longest = values.shape.index(max(values.shape))
    spots = []
    for shift in (0, 1):
        where = [jax.random.randint(jax.random.fold_in(rng, axis), (), 0, length) for axis, length in enumerate(values.shape)]
        where[longest] = (where[longest] + shift) % values.shape[longest]
        spots.append(tuple(where))
    return values.at[spots[0]].set(low).at[spots[1]].set(top_value)


def block_scale(own_key, dims, cuts, smallest, largest):
    factor_of, own = 1.0, jax.random.fold_in(own_key, 6)
    for axis_at, blocks in cuts:
        heights = jnp.exp(jax.random.uniform(jax.random.fold_in(own, axis_at), (blocks,), jnp.float32, smallest / len(cuts), largest / len(cuts)))
        factor_of = factor_of * jnp.repeat(heights, dims[axis_at] // blocks).reshape([-1 if axis == axis_at else 1 for axis in range(len(dims))])
    return factor_of


def setup_inputs(seed: int = 0) -> dict:
    keys = jax.random.split(jax.random.key(seed), 8)
    dist = draw_dist(jax.random.fold_in(keys[7], 71), 0)
    free_stream = draw_free_stream(jax.random.fold_in(keys[7], 71), 0)
    area_normal = draw_area_normal(jax.random.fold_in(keys[7], 71), 0)
    cell_volume = jnp.clip(jnp.exp(math.log(2.0) - 1.3862944 * jax.random.uniform(keys[3], (CELLS,), jnp.float32) ** block_scale(keys[3], (CELLS,), ((0, 32),), -0.2, 0.2)), 0.5, 2.0)
    face_nbr = place_ends(jax.random.randint(keys[4], (FACES, CELLS), 0, CELL_DEV + DIRS * SEND), jax.random.fold_in(keys[4], 1), 0, (CELL_DEV + DIRS * SEND) - 1).astype(jnp.int32)
    face_type = draw_face_type(jax.random.fold_in(keys[7], 71), 0)
    send_list = place_ends(jax.random.randint(keys[6], (DIRS, SEND * N_SPACE), 0, CELL_DEV), jax.random.fold_in(keys[6], 1), 0, CELL_DEV - 1).astype(jnp.int32)
    return {"dist": dist, "free_stream": free_stream, "area_normal": area_normal, "cell_volume": cell_volume, "face_nbr": face_nbr, "face_type": face_type, "send_list": send_list}


CFL = 0.9
MU_REF = 60.0
OMEGA = 0.81
PRANDTL = 2.0 / 3.0
neighbour_steps = (1, -1, 2, -2)

def grid_speeds(vel_index):
    spacing = 24.0 / NODES
    half = (NODES - 1) / 2.0
    first = (vel_index // (NODES * NODES)).astype(jnp.float32)
    second = (vel_index // NODES % NODES).astype(jnp.float32)
    last_axis = (vel_index % NODES).astype(jnp.float32)
    return ((first - half) * spacing, (second - half) * spacing, (last_axis - half) * spacing)

def source_columns(face_nbr, send_list):
    partition = (jnp.arange(CELLS, dtype=jnp.int32) // CELL_DEV)[None, :]
    local_face = face_nbr < CELL_DEV
    received = jnp.maximum(face_nbr - CELL_DEV, 0)
    direction = received // SEND
    within = received % SEND
    steps_table = jnp.array(neighbour_steps, dtype=jnp.int32)
    source_part = (partition - steps_table[direction]) % N_SPACE
    remote_cell = send_list[direction, source_part * SEND + within]
    return jnp.where(local_face, partition * CELL_DEV + face_nbr, source_part * CELL_DEV + remote_cell).astype(jnp.int32)

def hydrodynamic_variables(integral_averages):
    specific_matter_amount = integral_averages[0]
    mean_gas_speed = [integral_averages[1 + axis] / specific_matter_amount for axis in range(3)]
    particle_contribution = mean_gas_speed[0] ** 2 + mean_gas_speed[1] ** 2 + mean_gas_speed[2] ** 2
    local_thermal_level = (2.0 * integral_averages[4] / specific_matter_amount - particle_contribution) / 3.0
    return (specific_matter_amount, mean_gas_speed, local_thermal_level)

def reference(dist, free_stream, area_normal, cell_volume, face_nbr, face_type, send_list):
    speeds = grid_speeds(jnp.arange(VELS, dtype=jnp.int32))
    spacing = 24.0 / NODES
    weight = spacing ** 3
    top_speed = (NODES - 1) / 2.0 * spacing * math.sqrt(3.0)
    normals = area_normal.reshape(FACES, 3, CELLS)
    face_areas = jnp.sqrt(lax.optimization_barrier(jnp.sum(normals * normals, axis=1)))
    cell_limit = cell_volume / (top_speed * lax.optimization_barrier(jnp.sum(face_areas, axis=0)))
    time_step = CFL * jnp.min(cell_limit)
    step_ratio = time_step / cell_volume
    sources = source_columns(face_nbr, send_list)
    columns = [speeds[axis][:, None] for axis in range(3)]
    speed_sq = columns[0] ** 2 + columns[1] ** 2 + columns[2] ** 2

    def moments_of(field):
        return jnp.stack([weight * lax.optimization_barrier(jnp.sum(field, axis=0)), weight * lax.optimization_barrier(jnp.sum(columns[0] * field, axis=0)), weight * lax.optimization_barrier(jnp.sum(columns[1] * field, axis=0)), weight * lax.optimization_barrier(jnp.sum(columns[2] * field, axis=0)), weight * lax.optimization_barrier(jnp.sum(0.5 * speed_sq * field, axis=0))])

    def one_part(partition_id):
        start = partition_id * CELL_DEV
        own_cells = lax.dynamic_slice_in_dim(dist, start, CELL_DEV, 1)
        block_sources = lax.dynamic_slice_in_dim(sources, start, CELL_DEV, 1)
        block_normals = lax.dynamic_slice_in_dim(normals, start, CELL_DEV, 2)
        block_kinds = lax.dynamic_slice_in_dim(face_type, start, CELL_DEV, 1)
        block_ratio = lax.dynamic_slice_in_dim(step_ratio, start, CELL_DEV, 0)
        flux_total = jnp.zeros_like(own_cells)
        for face_slot in range(FACES):
            normal_speed = columns[0] * block_normals[face_slot, 0] + columns[1] * block_normals[face_slot, 1] + columns[2] * block_normals[face_slot, 2]
            outside = jnp.take(dist, block_sources[face_slot], axis=1)
            face_kind = block_kinds[face_slot]
            outside = jnp.where(face_kind == 0, outside, jnp.where(face_kind == 1, free_stream[:, None], own_cells))
            flux_total = flux_total + jnp.where(normal_speed > 0, normal_speed * own_cells, normal_speed * outside)
        invariant_quantities = moments_of(own_cells)
        specific_matter_amount, mean_gas_speed, local_thermal_level = hydrodynamic_variables(invariant_quantities)
        rel_old = [columns[axis] - mean_gas_speed[axis] for axis in range(3)]
        rel_old_sq = rel_old[0] ** 2 + rel_old[1] ** 2 + rel_old[2] ** 2
        heat_flux = [0.5 * weight * lax.optimization_barrier(jnp.sum(rel_old[axis] * rel_old_sq * own_cells, axis=0)) for axis in range(3)]
        new_moments = invariant_quantities - block_ratio[None, :] * moments_of(flux_total)
        density_new, mean_new, temp_new = hydrodynamic_variables(new_moments)
        relax_time = MU_REF * temp_new ** OMEGA / (density_new * temp_new)
        relax_ratio = time_step / relax_time
        rel_new = [columns[axis] - mean_new[axis] for axis in range(3)]
        rel_sq = rel_new[0] ** 2 + rel_new[1] ** 2 + rel_new[2] ** 2
        maxwell = density_new * (2.0 * math.pi * temp_new) ** (-1.5) * jnp.exp(-rel_sq / (2.0 * temp_new))
        along_heat = rel_new[0] * heat_flux[0] + rel_new[1] * heat_flux[1] + rel_new[2] * heat_flux[2]
        shakhov = maxwell * (1.0 + (1.0 - PRANDTL) * along_heat / (5.0 * density_new * temp_new * temp_new) * (rel_sq / temp_new - 5.0))
        transported = own_cells - block_ratio[None, :] * flux_total
        return (transported + relax_ratio * shakhov) / (1.0 + relax_ratio)
    blocks = lax.map(one_part, jnp.arange(N_SPACE, dtype=jnp.int32))
    return jnp.moveaxis(blocks, 0, 1).reshape(VELS, CELLS)
```

```python
import functools
import math

import jax
import jax.numpy as jnp
from jax import lax
from jax.experimental import pallas as pl
from jax.experimental.pallas import tpu as pltpu
from jax.sharding import PartitionSpec as P

MESH = pl.DeviceIdType.MESH
F32 = jnp.float32
BF16 = jnp.bfloat16

NODES = 24
HALF = (NODES - 1) / 2.0
TOP_SPEED = HALF * math.sqrt(3.0)
CFL = 0.9
MU_REF = 60.0
OMEGA = 0.81
PRANDTL = 2.0 / 3.0
STEPS = (1, -1, 2, -2)

VELS = 1728
CELLS = 512
SEND = 128
CHUNK = 144
CHUNKS = VELS // CHUNK
GROUPS = CHUNK // NODES


def two_parts(x):
    high = x.astype(BF16)
    low = (x - high.astype(F32)).astype(BF16)
    return high, low


def fold(x):
    return x[0:8] + x[8:16] + x[16:24]


def group_speeds(vel, group):
    first = (vel * 3 + group // NODES).astype(F32) - HALF
    second = (group % NODES).astype(F32) - HALF
    return first, second


def one_hot(rows, base, wanted):
    ids = lax.broadcasted_iota(jnp.int32, (rows, wanted.shape[1]), 0) + base
    return jnp.where(ids == wanted, 1.0, 0.0).astype(BF16)


def transport(
    n_space,
    dist_hbm,
    stream_ref,
    area_ref,
    volume_ref,
    nbr_ref,
    type_ref,
    list_ref,
    moved,
    coef_ref,
    dist_v,
    parts,
    outgoing,
    arrived,
    picks,
    send_picks,
    gathered,
    arrived_parts,
    normal,
    slope,
    inflow,
    source,
    stream_b,
    sums,
    old_msg,
    old_in,
    old_msg2,
    old_in2,
    new_msg,
    new_in,
    min_msg,
    min_in,
    min_msg2,
    min_in2,
    load_sem,
    send_sem,
    recv_sem,
    small_send,
    small_recv,
):
    s = lax.axis_index("space")
    v = lax.axis_index("vel")
    near = 8
    far = n_space // near
    partners = [lax.rem(s + step + n_space, n_space) for step in STEPS]
    near_peers = [(s // near) * near + lax.rem(s + i, near) for i in range(1, near)]
    far_peers = [lax.rem(s + near * i, n_space) for i in range(1, far)]
    vel_peers = [lax.rem(v + i, 8) for i in range(1, 8)]
    x_peers = [lax.rem(v + 2 * i, 8) for i in range(1, 4)]
    z_peer = v + 1 - 2 * lax.rem(v, 2)

    barrier = pltpu.get_barrier_semaphore()
    greeted = [(q, v) for q in partners + near_peers + far_peers]
    greeted += [(s, q) for q in vel_peers]
    for q in greeted:
        pl.semaphore_signal(barrier, inc=1, device_id=q, device_id_type=MESH)

    def load(c):
        rows = pl.ds(pl.multiple_of(c * CHUNK, CHUNK), CHUNK)
        return pltpu.make_async_copy(dist_hbm.at[rows], dist_v.at[rows], load_sem.at[c])

    def send(c, d):
        rows = pl.ds(pl.multiple_of(c * CHUNK, CHUNK), CHUNK)
        return pltpu.make_async_remote_copy(
            src_ref=outgoing.at[d, rows],
            dst_ref=arrived.at[d, rows],
            send_sem=send_sem.at[c, d],
            recv_sem=recv_sem.at[c, d],
            device_id=(partners[d], v),
            device_id_type=MESH,
        )

    def small(src, dst, at, where):
        return pltpu.make_async_remote_copy(
            src_ref=src,
            dst_ref=dst,
            send_sem=small_send.at[at],
            recv_sem=small_recv.at[at],
            device_id=where,
            device_id_type=MESH,
        )

    near_copies = [
        small(min_msg, min_in.at[i], i, (near_peers[i], v)) for i in range(near - 1)
    ]
    far_copies = [
        small(min_msg2, min_in2.at[i], 7 + i, (far_peers[i], v)) for i in range(far - 1)
    ]
    x_copies = [small(old_msg, old_in.at[i], 10 + i, (s, x_peers[i])) for i in range(3)]
    z_copy = small(old_msg2, old_in2, 13, (s, z_peer))
    new_copies = [
        small(new_msg, new_in.at[i], 14 + i, (s, vel_peers[i])) for i in range(7)
    ]

    for c in range(CHUNKS):
        load(c).start()

    send_picks[...] = one_hot(
        CELLS, 0, jnp.concatenate([list_ref[d : d + 1, :] for d in range(4)], axis=1)
    )

    def pack(c):
        rows = pl.ds(pl.multiple_of(c * CHUNK, CHUNK), CHUNK)
        high, low = two_parts(dist_v[rows, :])
        parts[c, 0:CHUNK, :] = high
        parts[c, CHUNK : 2 * CHUNK, :] = low
        both = jnp.dot(parts[c], send_picks[...], preferred_element_type=F32)
        picked = both[0:CHUNK] + both[CHUNK : 2 * CHUNK]
        for d in range(4):
            outgoing[d, rows, :] = picked[:, d * SEND : (d + 1) * SEND]

    load(0).wait()
    pack(0)
    pl.semaphore_wait(barrier, len(greeted))
    for d in range(4):
        send(0, d).start()

    def pack_and_send(c, _):
        load(c).wait()
        pack(c)
        for d in range(4):
            send(c, d).start()
        return 0

    lax.fori_loop(1, CHUNKS, pack_and_send, 0)

    normal[...] = jnp.zeros_like(normal)
    for k in range(6):
        for axis in range(3):
            normal[axis, k : k + 1, :] = area_ref[3 * k + axis : 3 * k + axis + 1, :]
    areas = jnp.sqrt(normal[0] * normal[0] + normal[1] * normal[1] + normal[2] * normal[2])
    volume = volume_ref[...]
    limit = volume / (TOP_SPEED * jnp.sum(areas, axis=0, keepdims=True))
    least = jnp.minimum(
        jnp.minimum(limit[:, 0:128], limit[:, 128:256]),
        jnp.minimum(limit[:, 256:384], limit[:, 384:512]),
    )
    min_msg[...] = jnp.broadcast_to(least, (8, 128))
    for copy in near_copies:
        copy.start()

    speed = lax.broadcasted_iota(jnp.int32, (NODES, CELLS), 0).astype(F32) - HALF
    for k in range(6):
        slope[k] = speed * normal[2, k : k + 1, :]
    for axis in range(3):
        normal[axis, 6:7, :] = jnp.sum(normal[axis, 0:6, :], axis=0, keepdims=True)
    slope[6] = speed * normal[2, 6:7, :]
    kind = type_ref[...]
    cell_ids = lax.broadcasted_iota(jnp.int32, (6, CELLS), 1)
    source[0:6, :] = jnp.where(kind == 0, nbr_ref[...], jnp.where(kind == 2, cell_ids, -1))
    inflow[0:6, :] = jnp.where(kind == 1, 1.0, 0.0)

    for i in range(14):
        start = min(i * 128, VELS - 128)
        row = stream_ref[:, start : start + 128]
        stream_b[start : start + 128, :] = jnp.broadcast_to(row, (128, 128)).T

    def fill(i, _):
        k = i // 8
        base = (i % 8) * 128
        picks[k, pl.ds(pl.multiple_of(base, 128), 128), :] = one_hot(
            128, base, source[pl.ds(k, 1), :]
        )
        return 0

    lax.fori_loop(0, 48, fill, 0)

    sums[...] = jnp.zeros_like(sums)

    def old_moments(group, _):
        rows = pl.ds(pl.multiple_of(group * NODES, NODES), NODES)
        cx, cy = group_speeds(v, group)
        d = dist_v[rows, :]
        d1 = d * speed
        d2 = d1 * speed
        d3 = d2 * speed
        s0, s1, s2, s3 = fold(d), fold(d1), fold(d2), fold(d3)
        sq = cx * cx + cy * cy
        r0 = sq * s0 + s2
        terms = (
            s0,
            cx * s0,
            cy * s0,
            s1,
            (cx * cx) * s0,
            (cy * cy) * s0,
            s2,
            (cx * cy) * s0,
            cx * s1,
            cy * s1,
            cx * r0,
            cy * r0,
            sq * s1 + s3,
        )
        for i, term in enumerate(terms):
            sums[i] += term
        return 0

    lax.fori_loop(0, VELS // NODES, old_moments, 0)
    old_msg[...] = jnp.zeros_like(old_msg)
    for i in range(13):
        old_msg[i : i + 1, :] = jnp.sum(sums[i], axis=0, keepdims=True)
    for copy in x_copies:
        copy.start()
    for copy in near_copies:
        copy.wait()
    lowest = min_msg[...]
    for i in range(near - 1):
        lowest = jnp.minimum(lowest, min_in[i])
    min_msg2[...] = lowest
    for copy in far_copies:
        copy.start()

    def products(lhs, half):
        for k in range(6):
            gathered[k] = jnp.dot(
                lhs, picks[k, half * CELLS : (half + 1) * CELLS, :], preferred_element_type=F32
            )

    def picked_rows(k, g):
        one = pl.ds(pl.multiple_of(g * NODES, NODES), NODES)
        two = pl.ds(pl.multiple_of(CHUNK + g * NODES, NODES), NODES)
        return gathered[k, one, :] + gathered[k, two, :]

    def normal_speed(k, cx, cy):
        return (cx * normal[0, k : k + 1, :] + cy * normal[1, k : k + 1, :]) + slope[k]

    def local_flux(c, _):
        products(parts[c], 0)

        def one_group(g, _):
            group = c * GROUPS + g
            rows = pl.ds(pl.multiple_of(group * NODES, NODES), NODES)
            cx, cy = group_speeds(v, group)
            inward = jnp.zeros((NODES, CELLS), F32)
            free = jnp.zeros((NODES, CELLS), F32)
            total = jnp.zeros((NODES, CELLS), F32)
            for k in range(6):
                u = jnp.minimum(normal_speed(k, cx, cy), 0.0)
                inward += u
                free += u * inflow[k : k + 1, :]
                total += u * picked_rows(k, g)
            stream = stream_b[rows, :]
            stream = jnp.concatenate([stream] * 4, axis=1)
            outward = normal_speed(6, cx, cy) - inward
            moved[rows, :] = outward * dist_v[rows, :] + total + free * stream
            return 0

        lax.fori_loop(0, GROUPS, one_group, 0)
        return 0

    lax.fori_loop(0, CHUNKS, local_flux, 0)

    for copy in x_copies:
        copy.wait()
    old_msg2[...] = old_msg[...] + old_in[0] + old_in[1] + old_in[2]
    z_copy.start()
    for copy in far_copies:
        copy.wait()
    lowest = min_msg2[...]
    for i in range(far - 1):
        lowest = jnp.minimum(lowest, min_in2[i])
    time_step = CFL * jnp.min(lowest[0:1, :], axis=1, keepdims=True)
    time_step = jnp.broadcast_to(time_step, (1, CELLS))
    ratio = time_step / volume

    for i in range(5):
        sums[i] = jnp.zeros((8, CELLS), F32)

    def remote_flux(c, _):
        rows = pl.ds(pl.multiple_of(c * CHUNK, CHUNK), CHUNK)
        for d in range(4):
            send(c, d).wait_recv()
        for d in range(4):
            high, low = two_parts(arrived[d, rows, :])
            lanes = slice(d * SEND, (d + 1) * SEND)
            arrived_parts[0:CHUNK, lanes] = high
            arrived_parts[CHUNK : 2 * CHUNK, lanes] = low
        products(arrived_parts[...], 1)

        def one_group(g, _):
            group = c * GROUPS + g
            own = pl.ds(pl.multiple_of(group * NODES, NODES), NODES)
            cx, cy = group_speeds(v, group)
            total = moved[own, :]
            for k in range(6):
                u = jnp.minimum(normal_speed(k, cx, cy), 0.0)
                total += u * picked_rows(k, g)
            t = dist_v[own, :] - ratio * total
            moved[own, :] = t
            t1 = t * speed
            s0, s1, s2 = fold(t), fold(t1), fold(t1 * speed)
            sums[0] += s0
            sums[1] += cx * s0
            sums[2] += cy * s0
            sums[3] += s1
            sums[4] += 0.5 * ((cx * cx + cy * cy) * s0 + s2)
            return 0

        lax.fori_loop(0, GROUPS, one_group, 0)
        return 0

    lax.fori_loop(0, CHUNKS, remote_flux, 0)

    new_msg[...] = jnp.zeros_like(new_msg)
    for i in range(5):
        new_msg[i : i + 1, :] = jnp.sum(sums[i], axis=0, keepdims=True)
    for copy in new_copies:
        copy.start()

    z_copy.wait()
    old = old_msg2[...] + old_in2[...]
    rho = old[0:1]
    mean = [old[1 + i : 2 + i] / rho for i in range(3)]
    pressure = [[old[4:5], old[7:8], old[8:9]], [old[7:8], old[5:6], old[9:10]], [old[8:9], old[9:10], old[6:7]]]
    trace = old[4:5] + old[5:6] + old[6:7]
    mean_sq = mean[0] * mean[0] + mean[1] * mean[1] + mean[2] * mean[2]
    for i in range(3):
        along = (
            mean[0] * pressure[i][0] + mean[1] * pressure[i][1] + mean[2] * pressure[i][2]
        )
        coef_ref[8 + i : 9 + i, :] = 0.5 * (
            old[10 + i : 11 + i] - 2.0 * along - mean[i] * trace + 2.0 * rho * mean_sq * mean[i]
        )
    coef_ref[11:12, :] = time_step
    coef_ref[12:16, :] = jnp.zeros((4, CELLS), F32)

    def finish_sends(c, _):
        for d in range(4):
            send(c, d).wait_send()
        return 0

    lax.fori_loop(0, CHUNKS, finish_sends, 0)
    for copy in new_copies:
        copy.wait()
    total = new_msg[...]
    for i in range(7):
        total = total + new_in[i]
    coef_ref[0:8, :] = total


def relax(moved, coef_ref, out_hbm, result, first, second, third, sem):
    v = lax.axis_index("vel")
    rho = coef_ref[0:1, :]
    mean = [coef_ref[1 + i : 2 + i, :] / rho for i in range(3)]
    heat = [coef_ref[8 + i : 9 + i, :] for i in range(3)]
    time_step = coef_ref[11:12, :]
    mean_sq = mean[0] * mean[0] + mean[1] * mean[1] + mean[2] * mean[2]
    temp = (2.0 * coef_ref[4:5, :] / rho - mean_sq) / 3.0
    relax_time = MU_REF * jnp.exp(OMEGA * jnp.log(temp)) / (rho * temp)
    relax_ratio = time_step / relax_time
    keep = 1.0 / (1.0 + relax_ratio)
    cold = 1.0 / temp
    root = lax.rsqrt(2.0 * math.pi * temp)
    scale = relax_ratio * keep * rho * (root * root * root)
    bend = (1.0 - PRANDTL) / (5.0 * rho * temp * temp)
    speed = lax.broadcasted_iota(jnp.int32, (NODES, CELLS), 0).astype(F32) - HALF
    for axis, table in ((1, second), (2, third)):
        rel = speed - mean[axis]
        sq = rel * rel * cold
        table[0] = jnp.exp(-0.5 * sq)
        table[1] = sq
        table[2] = rel * (heat[axis] * bend)
    own = lax.broadcasted_iota(jnp.int32, (8, CELLS), 0).astype(F32) - HALF
    rel = own + (v * 3).astype(F32) - mean[0]
    sq = rel * rel * cold
    first[0] = jnp.exp(-0.5 * sq) * scale
    first[1] = sq - 5.0
    first[2] = rel * (heat[0] * bend)

    def one_chunk(c, _):
        def one_group(g, _):
            group = c * GROUPS + g
            rows = pl.ds(pl.multiple_of(group * NODES, NODES), NODES)
            a = pl.ds(group // NODES, 1)
            b = pl.ds(group % NODES, 1)
            weight = first[0, a, :] * second[0, b, :]
            sq = (first[1, a, :] + second[1, b, :]) + third[1]
            along = (first[2, a, :] + second[2, b, :]) + third[2]
            gauss = weight * third[0]
            result[rows, :] = moved[rows, :] * keep + gauss * (1.0 + along * sq)
            return 0

        lax.fori_loop(0, GROUPS, one_group, 0)
        rows = pl.ds(pl.multiple_of(c * CHUNK, CHUNK), CHUNK)
        pltpu.make_async_copy(result.at[rows], out_hbm.at[rows], sem.at[c]).start()
        return 0

    lax.fori_loop(0, CHUNKS, one_chunk, 0)

    def finish(c, _):
        rows = pl.ds(pl.multiple_of(c * CHUNK, CHUNK), CHUNK)
        pltpu.make_async_copy(result.at[rows], out_hbm.at[rows], sem.at[c]).wait()
        return 0

    lax.fori_loop(0, CHUNKS, finish, 0)


def solution(mesh):
    n_space = mesh.shape["space"]
    vmem = pl.BlockSpec(memory_space=pltpu.VMEM)
    hbm = pl.BlockSpec(memory_space=pl.ANY)

    def local(dist, free_stream, area_normal, cell_volume, face_nbr, face_type, send_list):
        moved, coef = pl.pallas_call(
            functools.partial(transport, n_space),
            out_shape=(
                jax.ShapeDtypeStruct((VELS, CELLS), F32),
                jax.ShapeDtypeStruct((16, CELLS), F32),
            ),
            in_specs=[hbm] + [vmem] * 6,
            out_specs=(vmem, vmem),
            scratch_shapes=[
                pltpu.VMEM((VELS, CELLS), F32),
                pltpu.VMEM((CHUNKS, 2 * CHUNK, CELLS), BF16),
                pltpu.VMEM((4, VELS, SEND), F32),
                pltpu.VMEM((4, VELS, SEND), F32),
                pltpu.VMEM((6, 2 * CELLS, CELLS), BF16),
                pltpu.VMEM((CELLS, CELLS), BF16),
                pltpu.VMEM((6, 2 * CHUNK, CELLS), F32),
                pltpu.VMEM((2 * CHUNK, CELLS), BF16),
                pltpu.VMEM((3, 8, CELLS), F32),
                pltpu.VMEM((7, NODES, CELLS), F32),
                pltpu.VMEM((8, CELLS), F32),
                pltpu.VMEM((8, CELLS), jnp.int32),
                pltpu.VMEM((VELS, 128), F32),
                pltpu.VMEM((13, 8, CELLS), F32),
                pltpu.VMEM((16, CELLS), F32),
                pltpu.VMEM((3, 16, CELLS), F32),
                pltpu.VMEM((16, CELLS), F32),
                pltpu.VMEM((16, CELLS), F32),
                pltpu.VMEM((8, CELLS), F32),
                pltpu.VMEM((7, 8, CELLS), F32),
                pltpu.VMEM((8, 128), F32),
                pltpu.VMEM((7, 8, 128), F32),
                pltpu.VMEM((8, 128), F32),
                pltpu.VMEM((max(1, n_space // 8 - 1), 8, 128), F32),
                pltpu.SemaphoreType.DMA((CHUNKS,)),
                pltpu.SemaphoreType.DMA((CHUNKS, 4)),
                pltpu.SemaphoreType.DMA((CHUNKS, 4)),
                pltpu.SemaphoreType.DMA((21,)),
                pltpu.SemaphoreType.DMA((21,)),
            ],
            compiler_params=pltpu.CompilerParams(
                collective_id=0, has_side_effects=True, vmem_limit_bytes=44 * 2**20
            ),
            name="transport",
        )(
            dist,
            free_stream.reshape(1, VELS),
            area_normal,
            cell_volume.reshape(1, CELLS),
            face_nbr,
            face_type,
            send_list,
        )
        return pl.pallas_call(
            relax,
            out_shape=jax.ShapeDtypeStruct((VELS, CELLS), F32),
            in_specs=[vmem, vmem],
            out_specs=hbm,
            scratch_shapes=[
                pltpu.VMEM((VELS, CELLS), F32),
                pltpu.VMEM((3, 8, CELLS), F32),
                pltpu.VMEM((3, NODES, CELLS), F32),
                pltpu.VMEM((3, NODES, CELLS), F32),
                pltpu.SemaphoreType.DMA((CHUNKS,)),
            ],
            compiler_params=pltpu.CompilerParams(vmem_limit_bytes=24 * 2**20),
            name="relax",
        )(moved, coef)

    return jax.shard_map(
        local,
        mesh=mesh,
        in_specs=(
            P("vel", "space"),
            P("vel"),
            P(None, "space"),
            P("space"),
            P(None, "space"),
            P(None, "space"),
            P(None, "space"),
        ),
        out_specs=P("vel", "space"),
        check_vma=False,
    )
```

```python
import functools
import math

import jax
import jax.numpy as jnp
from jax import lax
from jax.experimental import pallas as pl
from jax.experimental.pallas import tpu as pltpu
from jax.sharding import PartitionSpec as P

MESH = pl.DeviceIdType.MESH
F32 = jnp.float32
BF16 = jnp.bfloat16

NODES = 24
HALF = (NODES - 1) / 2.0
TOP_SPEED = HALF * math.sqrt(3.0)
CFL = 0.9
MU_REF = 60.0
OMEGA = 0.81
PRANDTL = 2.0 / 3.0
STEPS = (1, -1, 2, -2)

VELS = 1728
CELLS = 512
SEND = 128
CHUNK = 144
CHUNKS = VELS // CHUNK
GROUPS = CHUNK // NODES
WINDOW = 3
AHEAD = 2


def two_parts(x):
    high = x.astype(BF16)
    low = (x - high.astype(F32)).astype(BF16)
    return high, low


def fold(x):
    return x[0:8] + x[8:16] + x[16:24]


def group_speeds(vel, group):
    first = (vel * 3 + group // NODES).astype(F32) - HALF
    second = (group % NODES).astype(F32) - HALF
    return first, second


def one_hot(rows, base, wanted):
    ids = lax.broadcasted_iota(jnp.int32, (rows, wanted.shape[1]), 0) + base
    return jnp.where(ids == wanted, 1.0, 0.0).astype(BF16)


def transport(
    n_space,
    dist_hbm,
    stream_hbm,
    area_hbm,
    volume_hbm,
    nbr_hbm,
    type_hbm,
    list_hbm,
    moved,
    coef_ref,
    stream_ref,
    area_ref,
    volume_ref,
    nbr_ref,
    type_ref,
    list_ref,
    dist_v,
    parts,
    outgoing,
    arrived,
    picks,
    send_picks,
    gathered,
    arrived_parts,
    normal,
    slope,
    inflow,
    source,
    stream_b,
    sums,
    old_msg,
    old_in,
    old_msg2,
    old_in2,
    new_msg,
    new_in,
    min_msg,
    min_in,
    min_msg2,
    min_in2,
    load_sem,
    input_sem,
    send_sem,
    recv_sem,
    small_send,
    small_recv,
):
    s = lax.axis_index("space")
    v = lax.axis_index("vel")
    near = 8
    far = n_space // near
    partners = [lax.rem(s + step + n_space, n_space) for step in STEPS]
    near_peers = [(s // near) * near + lax.rem(s + i, near) for i in range(1, near)]
    far_peers = [lax.rem(s + near * i, n_space) for i in range(1, far)]
    vel_peers = [lax.rem(v + i, 8) for i in range(1, 8)]
    x_peers = [lax.rem(v + 2 * i, 8) for i in range(1, 4)]
    z_peer = v + 1 - 2 * lax.rem(v, 2)

    barrier = pltpu.get_barrier_semaphore()
    greeted = [(q, v) for q in partners + near_peers + far_peers]
    greeted += [(s, q) for q in vel_peers]
    for q in greeted:
        pl.semaphore_signal(barrier, inc=1, device_id=q, device_id_type=MESH)

    def load(c):
        rows = pl.ds(pl.multiple_of(c * CHUNK, CHUNK), CHUNK)
        return pltpu.make_async_copy(dist_hbm.at[rows], dist_v.at[rows], load_sem.at[c])

    def send(c, d):
        rows = pl.ds(pl.multiple_of(c * CHUNK, CHUNK), CHUNK)
        return pltpu.make_async_remote_copy(
            src_ref=outgoing.at[d, rows],
            dst_ref=arrived.at[d, rows],
            send_sem=send_sem.at[c, d],
            recv_sem=recv_sem.at[c, d],
            device_id=(partners[d], v),
            device_id_type=MESH,
        )

    def small(src, dst, at, where):
        return pltpu.make_async_remote_copy(
            src_ref=src,
            dst_ref=dst,
            send_sem=small_send.at[at],
            recv_sem=small_recv.at[at],
            device_id=where,
            device_id_type=MESH,
        )

    near_copies = [
        small(min_msg, min_in.at[i], i, (near_peers[i], v)) for i in range(near - 1)
    ]
    far_copies = [
        small(min_msg2, min_in2.at[i], 7 + i, (far_peers[i], v)) for i in range(far - 1)
    ]
    x_copies = [small(old_msg, old_in.at[i], 10 + i, (s, x_peers[i])) for i in range(3)]
    z_copy = small(old_msg2, old_in2, 13, (s, z_peer))
    new_copies = [
        small(new_msg, new_in.at[i], 14 + i, (s, vel_peers[i])) for i in range(7)
    ]

    inputs = [
        pltpu.make_async_copy(src, dst, input_sem.at[i])
        for i, (src, dst) in enumerate(
            (
                (list_hbm, list_ref),
                (area_hbm, area_ref),
                (volume_hbm, volume_ref),
                (nbr_hbm, nbr_ref),
                (type_hbm, type_ref),
                (stream_hbm, stream_ref),
            )
        )
    ]
    inputs[0].start()
    load(0).start()
    for copy in inputs[1:]:
        copy.start()
    for c in range(1, CHUNKS):
        load(c).start()

    inputs[0].wait()
    send_picks[...] = one_hot(
        CELLS, 0, jnp.concatenate([list_ref[d : d + 1, :] for d in range(4)], axis=1)
    )

    def pack(c):
        rows = pl.ds(pl.multiple_of(c * CHUNK, CHUNK), CHUNK)
        high, low = two_parts(dist_v[rows, :])
        parts[c, 0:CHUNK, :] = high
        parts[c, CHUNK : 2 * CHUNK, :] = low
        both = jnp.dot(parts[c], send_picks[...], preferred_element_type=F32)
        picked = both[0:CHUNK] + both[CHUNK : 2 * CHUNK]
        for d in range(4):
            outgoing[d, rows, :] = picked[:, d * SEND : (d + 1) * SEND]

    def start_sends(c):
        for d in range(4):
            send(c, d).start()

    load(0).wait()
    pack(0)
    for copy in inputs[1:]:
        copy.wait()
    normal[...] = jnp.zeros_like(normal)
    for k in range(6):
        for axis in range(3):
            normal[axis, k : k + 1, :] = area_ref[3 * k + axis : 3 * k + axis + 1, :]
    areas = jnp.sqrt(normal[0] * normal[0] + normal[1] * normal[1] + normal[2] * normal[2])
    volume = volume_ref[...].reshape(1, CELLS)
    limit = volume / (TOP_SPEED * jnp.sum(areas, axis=0, keepdims=True))
    least = jnp.minimum(
        jnp.minimum(limit[:, 0:128], limit[:, 128:256]),
        jnp.minimum(limit[:, 256:384], limit[:, 384:512]),
    )
    min_msg[...] = jnp.broadcast_to(least, (8, 128))

    pl.semaphore_wait(barrier, len(greeted))
    for copy in near_copies:
        copy.start()
    start_sends(0)

    def pack_next(c, _):
        load(c).wait()
        pack(c)

        @pl.when(c < WINDOW)
        def _():
            start_sends(c)

        return 0

    lax.fori_loop(1, CHUNKS, pack_next, 0)

    speed = lax.broadcasted_iota(jnp.int32, (NODES, CELLS), 0).astype(F32) - HALF
    for k in range(6):
        slope[k] = speed * normal[2, k : k + 1, :]
    for axis in range(3):
        normal[axis, 6:7, :] = jnp.sum(normal[axis, 0:6, :], axis=0, keepdims=True)
    slope[6] = speed * normal[2, 6:7, :]
    kind = type_ref[...]
    cell_ids = lax.broadcasted_iota(jnp.int32, (6, CELLS), 1)
    source[0:6, :] = jnp.where(kind == 0, nbr_ref[...], jnp.where(kind == 2, cell_ids, -1))
    inflow[0:6, :] = jnp.where(kind == 1, 1.0, 0.0)

    for i in range(14):
        start = min(i * 128, VELS - 128)
        row = stream_ref[start : start + 128].reshape(1, 128)
        stream_b[start : start + 128, :] = jnp.broadcast_to(row, (128, 128)).T

    def fill(i, _):
        k = i // 8
        base = (i % 8) * 128
        picks[k, pl.ds(pl.multiple_of(base, 128), 128), :] = one_hot(
            128, base, source[pl.ds(k, 1), :]
        )
        return 0

    lax.fori_loop(0, 48, fill, 0)

    for copy in near_copies:
        copy.wait()
    lowest = min_msg[...]
    for i in range(near - 1):
        lowest = jnp.minimum(lowest, min_in[i])
    min_msg2[...] = lowest
    for copy in far_copies:
        copy.start()

    sums[...] = jnp.zeros_like(sums)

    def old_moments(group, _):
        rows = pl.ds(pl.multiple_of(group * NODES, NODES), NODES)
        cx, cy = group_speeds(v, group)
        d = dist_v[rows, :]
        d1 = d * speed
        d2 = d1 * speed
        d3 = d2 * speed
        s0, s1, s2, s3 = fold(d), fold(d1), fold(d2), fold(d3)
        sq = cx * cx + cy * cy
        r0 = sq * s0 + s2
        terms = (
            s0,
            cx * s0,
            cy * s0,
            s1,
            (cx * cx) * s0,
            (cy * cy) * s0,
            s2,
            (cx * cy) * s0,
            cx * s1,
            cy * s1,
            cx * r0,
            cy * r0,
            sq * s1 + s3,
        )
        for i, term in enumerate(terms):
            sums[i] += term
        return 0

    lax.fori_loop(0, VELS // NODES, old_moments, 0)
    old_msg[...] = jnp.zeros_like(old_msg)
    for i in range(13):
        old_msg[i : i + 1, :] = jnp.sum(sums[i], axis=0, keepdims=True)
    for copy in x_copies:
        copy.start()
    def products(lhs, half):
        for k in range(6):
            gathered[k] = jnp.dot(
                lhs, picks[k, half * CELLS : (half + 1) * CELLS, :], preferred_element_type=F32
            )

    def picked_rows(k, g):
        one = pl.ds(pl.multiple_of(g * NODES, NODES), NODES)
        two = pl.ds(pl.multiple_of(CHUNK + g * NODES, NODES), NODES)
        return gathered[k, one, :] + gathered[k, two, :]

    def normal_speed(k, cx, cy):
        return (cx * normal[0, k : k + 1, :] + cy * normal[1, k : k + 1, :]) + slope[k]

    def local_flux(c, _):
        products(parts[c], 0)

        def one_group(g, _):
            group = c * GROUPS + g
            rows = pl.ds(pl.multiple_of(group * NODES, NODES), NODES)
            cx, cy = group_speeds(v, group)
            inward = jnp.zeros((NODES, CELLS), F32)
            free = jnp.zeros((NODES, CELLS), F32)
            total = jnp.zeros((NODES, CELLS), F32)
            for k in range(6):
                u = jnp.minimum(normal_speed(k, cx, cy), 0.0)
                inward += u
                free += u * inflow[k : k + 1, :]
                total += u * picked_rows(k, g)
            stream = stream_b[rows, :]
            stream = jnp.concatenate([stream] * 4, axis=1)
            outward = normal_speed(6, cx, cy) - inward
            moved[rows, :] = outward * dist_v[rows, :] + total + free * stream
            return 0

        lax.fori_loop(0, GROUPS, one_group, 0)
        return 0

    lax.fori_loop(0, AHEAD, local_flux, 0)

    for copy in far_copies:
        copy.wait()
    lowest = min_msg2[...]
    for i in range(far - 1):
        lowest = jnp.minimum(lowest, min_in2[i])
    time_step = CFL * jnp.min(lowest[0:1, :], axis=1, keepdims=True)
    time_step = jnp.broadcast_to(time_step, (1, CELLS))
    ratio = time_step / volume

    for i in range(5):
        sums[i] = jnp.zeros((8, CELLS), F32)

    def remote_flux(c, _):
        rows = pl.ds(pl.multiple_of(c * CHUNK, CHUNK), CHUNK)

        @pl.when(c + AHEAD < CHUNKS)
        def _():
            local_flux(c + AHEAD, 0)

        for d in range(4):
            send(c, d).wait_recv()

        @pl.when(c + WINDOW < CHUNKS)
        def _():
            for d in range(4):
                send(c, d).wait_send()
            start_sends(c + WINDOW)

        @pl.when(c == 4)
        def _():
            for copy in x_copies:
                copy.wait()
            old_msg2[...] = old_msg[...] + old_in[0] + old_in[1] + old_in[2]
            z_copy.start()

        for d in range(4):
            high, low = two_parts(arrived[d, rows, :])
            lanes = slice(d * SEND, (d + 1) * SEND)
            arrived_parts[0:CHUNK, lanes] = high
            arrived_parts[CHUNK : 2 * CHUNK, lanes] = low
        products(arrived_parts[...], 1)

        def one_group(g, _):
            group = c * GROUPS + g
            own = pl.ds(pl.multiple_of(group * NODES, NODES), NODES)
            cx, cy = group_speeds(v, group)
            total = moved[own, :]
            for k in range(6):
                u = jnp.minimum(normal_speed(k, cx, cy), 0.0)
                total += u * picked_rows(k, g)
            t = dist_v[own, :] - ratio * total
            moved[own, :] = t
            t1 = t * speed
            s0, s1, s2 = fold(t), fold(t1), fold(t1 * speed)
            sums[0] += s0
            sums[1] += cx * s0
            sums[2] += cy * s0
            sums[3] += s1
            sums[4] += 0.5 * ((cx * cx + cy * cy) * s0 + s2)
            return 0

        lax.fori_loop(0, GROUPS, one_group, 0)
        return 0

    lax.fori_loop(0, CHUNKS, remote_flux, 0)

    new_msg[...] = jnp.zeros_like(new_msg)
    for i in range(5):
        new_msg[i : i + 1, :] = jnp.sum(sums[i], axis=0, keepdims=True)
    for copy in new_copies:
        copy.start()

    z_copy.wait()
    old = old_msg2[...] + old_in2[...]
    rho = old[0:1]
    mean = [old[1 + i : 2 + i] / rho for i in range(3)]
    pressure = [[old[4:5], old[7:8], old[8:9]], [old[7:8], old[5:6], old[9:10]], [old[8:9], old[9:10], old[6:7]]]
    trace = old[4:5] + old[5:6] + old[6:7]
    mean_sq = mean[0] * mean[0] + mean[1] * mean[1] + mean[2] * mean[2]
    for i in range(3):
        along = (
            mean[0] * pressure[i][0] + mean[1] * pressure[i][1] + mean[2] * pressure[i][2]
        )
        coef_ref[8 + i : 9 + i, :] = 0.5 * (
            old[10 + i : 11 + i] - 2.0 * along - mean[i] * trace + 2.0 * rho * mean_sq * mean[i]
        )
    coef_ref[11:12, :] = time_step
    coef_ref[12:16, :] = jnp.zeros((4, CELLS), F32)

    def finish_sends(c, _):
        for d in range(4):
            send(c, d).wait_send()
        return 0

    lax.fori_loop(CHUNKS - WINDOW, CHUNKS, finish_sends, 0)
    for copy in new_copies:
        copy.wait()
    total = new_msg[...]
    for i in range(7):
        total = total + new_in[i]
    coef_ref[0:8, :] = total


def relax(moved, coef_ref, out_hbm, result, first, second, third, sem):
    v = lax.axis_index("vel")
    rho = coef_ref[0:1, :]
    mean = [coef_ref[1 + i : 2 + i, :] / rho for i in range(3)]
    heat = [coef_ref[8 + i : 9 + i, :] for i in range(3)]
    time_step = coef_ref[11:12, :]
    mean_sq = mean[0] * mean[0] + mean[1] * mean[1] + mean[2] * mean[2]
    temp = (2.0 * coef_ref[4:5, :] / rho - mean_sq) / 3.0
    relax_time = MU_REF * jnp.exp(OMEGA * jnp.log(temp)) / (rho * temp)
    relax_ratio = time_step / relax_time
    keep = 1.0 / (1.0 + relax_ratio)
    cold = 1.0 / temp
    root = lax.rsqrt(2.0 * math.pi * temp)
    scale = relax_ratio * keep * rho * (root * root * root)
    bend = (1.0 - PRANDTL) / (5.0 * rho * temp * temp)
    speed = lax.broadcasted_iota(jnp.int32, (NODES, CELLS), 0).astype(F32) - HALF
    for axis, table in ((1, second), (2, third)):
        rel = speed - mean[axis]
        sq = rel * rel * cold
        table[0] = jnp.exp(-0.5 * sq)
        table[1] = sq
        table[2] = rel * (heat[axis] * bend)
    own = lax.broadcasted_iota(jnp.int32, (8, CELLS), 0).astype(F32) - HALF
    rel = own + (v * 3).astype(F32) - mean[0]
    sq = rel * rel * cold
    first[0] = jnp.exp(-0.5 * sq) * scale
    first[1] = sq - 5.0
    first[2] = rel * (heat[0] * bend)

    def one_chunk(c, _):
        def one_group(g, _):
            group = c * GROUPS + g
            rows = pl.ds(pl.multiple_of(group * NODES, NODES), NODES)
            a = pl.ds(group // NODES, 1)
            b = pl.ds(group % NODES, 1)
            weight = first[0, a, :] * second[0, b, :]
            sq = (first[1, a, :] + second[1, b, :]) + third[1]
            along = (first[2, a, :] + second[2, b, :]) + third[2]
            gauss = weight * third[0]
            result[rows, :] = moved[rows, :] * keep + gauss * (1.0 + along * sq)
            return 0

        lax.fori_loop(0, GROUPS, one_group, 0)
        rows = pl.ds(pl.multiple_of(c * CHUNK, CHUNK), CHUNK)
        pltpu.make_async_copy(result.at[rows], out_hbm.at[rows], sem.at[c]).start()
        return 0

    lax.fori_loop(0, CHUNKS, one_chunk, 0)

    def finish(c, _):
        rows = pl.ds(pl.multiple_of(c * CHUNK, CHUNK), CHUNK)
        pltpu.make_async_copy(result.at[rows], out_hbm.at[rows], sem.at[c]).wait()
        return 0

    lax.fori_loop(0, CHUNKS, finish, 0)


def solution(mesh):
    n_space = mesh.shape["space"]
    vmem = pl.BlockSpec(memory_space=pltpu.VMEM)
    hbm = pl.BlockSpec(memory_space=pl.ANY)
    raw = pl.BlockSpec(memory_space=pltpu.HBM)

    def local(dist, free_stream, area_normal, cell_volume, face_nbr, face_type, send_list):
        moved, coef = pl.pallas_call(
            functools.partial(transport, n_space),
            out_shape=(
                jax.ShapeDtypeStruct((VELS, CELLS), F32),
                jax.ShapeDtypeStruct((16, CELLS), F32),
            ),
            in_specs=[raw] * 7,
            out_specs=(vmem, vmem),
            scratch_shapes=[
                pltpu.VMEM((VELS,), F32),
                pltpu.VMEM((18, CELLS), F32),
                pltpu.VMEM((CELLS,), F32),
                pltpu.VMEM((6, CELLS), jnp.int32),
                pltpu.VMEM((6, CELLS), jnp.int32),
                pltpu.VMEM((4, SEND), jnp.int32),
                pltpu.VMEM((VELS, CELLS), F32),
                pltpu.VMEM((CHUNKS, 2 * CHUNK, CELLS), BF16),
                pltpu.VMEM((4, VELS, SEND), F32),
                pltpu.VMEM((4, VELS, SEND), F32),
                pltpu.VMEM((6, 2 * CELLS, CELLS), BF16),
                pltpu.VMEM((CELLS, CELLS), BF16),
                pltpu.VMEM((6, 2 * CHUNK, CELLS), F32),
                pltpu.VMEM((2 * CHUNK, CELLS), BF16),
                pltpu.VMEM((3, 8, CELLS), F32),
                pltpu.VMEM((7, NODES, CELLS), F32),
                pltpu.VMEM((8, CELLS), F32),
                pltpu.VMEM((8, CELLS), jnp.int32),
                pltpu.VMEM((VELS, 128), F32),
                pltpu.VMEM((13, 8, CELLS), F32),
                pltpu.VMEM((16, CELLS), F32),
                pltpu.VMEM((3, 16, CELLS), F32),
                pltpu.VMEM((16, CELLS), F32),
                pltpu.VMEM((16, CELLS), F32),
                pltpu.VMEM((8, CELLS), F32),
                pltpu.VMEM((7, 8, CELLS), F32),
                pltpu.VMEM((8, 128), F32),
                pltpu.VMEM((7, 8, 128), F32),
                pltpu.VMEM((8, 128), F32),
                pltpu.VMEM((max(1, n_space // 8 - 1), 8, 128), F32),
                pltpu.SemaphoreType.DMA((CHUNKS,)),
                pltpu.SemaphoreType.DMA((6,)),
                pltpu.SemaphoreType.DMA((CHUNKS, 4)),
                pltpu.SemaphoreType.DMA((CHUNKS, 4)),
                pltpu.SemaphoreType.DMA((21,)),
                pltpu.SemaphoreType.DMA((21,)),
            ],
            compiler_params=pltpu.CompilerParams(
                collective_id=0, has_side_effects=True, vmem_limit_bytes=44 * 2**20
            ),
            name="transport",
        )(
            *[
                pltpu.with_memory_space_constraint(x, pltpu.HBM)
                for x in (
                    dist,
                    free_stream,
                    area_normal,
                    cell_volume,
                    face_nbr,
                    face_type,
                    send_list,
                )
            ]
        )
        return pl.pallas_call(
            relax,
            out_shape=jax.ShapeDtypeStruct((VELS, CELLS), F32),
            in_specs=[vmem, vmem],
            out_specs=hbm,
            scratch_shapes=[
                pltpu.VMEM((VELS, CELLS), F32),
                pltpu.VMEM((3, 8, CELLS), F32),
                pltpu.VMEM((3, NODES, CELLS), F32),
                pltpu.VMEM((3, NODES, CELLS), F32),
                pltpu.SemaphoreType.DMA((CHUNKS,)),
            ],
            compiler_params=pltpu.CompilerParams(vmem_limit_bytes=24 * 2**20),
            name="relax",
        )(moved, coef)

    return jax.shard_map(
        local,
        mesh=mesh,
        in_specs=(
            P("vel", "space"),
            P("vel"),
            P(None, "space"),
            P("space"),
            P(None, "space"),
            P(None, "space"),
            P(None, "space"),
        ),
        out_specs=P("vel", "space"),
        check_vma=False,
    )
```

```python
import functools
import math

import jax
import jax.numpy as jnp
from jax import lax
from jax.experimental import pallas as pl
from jax.experimental.pallas import tpu as pltpu
from jax.sharding import PartitionSpec as P

MESH = pl.DeviceIdType.MESH
F32 = jnp.float32
BF16 = jnp.bfloat16

NODES = 24
HALF = (NODES - 1) / 2.0
TOP_SPEED = HALF * math.sqrt(3.0)
CFL = 0.9
MU_REF = 60.0
OMEGA = 0.81
PRANDTL = 2.0 / 3.0
STEPS = (1, -1, 2, -2)

VELS = 1728
CELLS = 512
SEND = 128
CHUNK = 144
CHUNKS = VELS // CHUNK
GROUPS = CHUNK // NODES
FIRST = 3
WINDOW = 12
SPLIT = 6


def two_parts(x):
    high = x.astype(BF16)
    low = (x - high.astype(F32)).astype(BF16)
    return high, low


def fold(x):
    return x[0:8] + x[8:16] + x[16:24]


def group_speeds(vel, group):
    first = (vel * 3 + group // NODES).astype(F32) - HALF
    second = (group % NODES).astype(F32) - HALF
    return first, second


def one_hot(rows, base, wanted):
    ids = lax.broadcasted_iota(jnp.int32, (rows, wanted.shape[1]), 0) + base
    return jnp.where(ids == wanted, 1.0, 0.0).astype(BF16)


def transport(
    n_space,
    dist_hbm,
    stream_hbm,
    area_hbm,
    volume_hbm,
    nbr_hbm,
    type_hbm,
    list_hbm,
    dist_v,
    moved,
    coef_ref,
    stream_ref,
    area_ref,
    volume_ref,
    nbr_ref,
    type_ref,
    list_ref,
    parts,
    outgoing,
    arrived,
    picks,
    send_picks,
    gathered,
    arrived_parts,
    normal,
    slope,
    inflow,
    source,
    stream_b,
    sums,
    old_msg,
    old_in,
    old_msg2,
    old_in2,
    new_msg,
    new_in,
    min_msg,
    min_in,
    min_msg2,
    min_in2,
    load_sem,
    input_sem,
    send_sem,
    recv_sem,
    small_send,
    small_recv,
):
    s = lax.axis_index("space")
    v = lax.axis_index("vel")
    near = 8
    far = n_space // near
    partners = [lax.rem(s + step + n_space, n_space) for step in STEPS]
    near_peers = [(s // near) * near + lax.rem(s + i, near) for i in range(1, near)]
    far_peers = [lax.rem(s + near * i, n_space) for i in range(1, far)]
    vel_peers = [lax.rem(v + i, 8) for i in range(1, 8)]
    x_peers = [lax.rem(v + 2 * i, 8) for i in range(1, 4)]
    z_peer = v + 1 - 2 * lax.rem(v, 2)

    barrier = pltpu.get_barrier_semaphore()
    greeted = [(q, v) for q in partners + near_peers + far_peers]
    greeted += [(s, q) for q in vel_peers]
    for q in greeted:
        pl.semaphore_signal(barrier, inc=1, device_id=q, device_id_type=MESH)

    def load(c):
        rows = pl.ds(pl.multiple_of(c * CHUNK, CHUNK), CHUNK)
        return pltpu.make_async_copy(dist_hbm.at[rows], dist_v.at[rows], load_sem.at[c])

    def send(c, d):
        rows = pl.ds(pl.multiple_of(c * CHUNK, CHUNK), CHUNK)
        return pltpu.make_async_remote_copy(
            src_ref=outgoing.at[d, rows],
            dst_ref=arrived.at[d, rows],
            send_sem=send_sem.at[c, d],
            recv_sem=recv_sem.at[c, d],
            device_id=(partners[d], v),
            device_id_type=MESH,
        )

    def small(src, dst, at, where):
        return pltpu.make_async_remote_copy(
            src_ref=src,
            dst_ref=dst,
            send_sem=small_send.at[at],
            recv_sem=small_recv.at[at],
            device_id=where,
            device_id_type=MESH,
        )

    near_copies = [
        small(min_msg, min_in.at[i], i, (near_peers[i], v)) for i in range(near - 1)
    ]
    far_copies = [
        small(min_msg2, min_in2.at[i], 7 + i, (far_peers[i], v)) for i in range(far - 1)
    ]
    x_copies = [small(old_msg, old_in.at[i], 10 + i, (s, x_peers[i])) for i in range(3)]
    z_copy = small(old_msg2, old_in2, 13, (s, z_peer))
    new_copies = [
        small(new_msg, new_in.at[i], 14 + i, (s, vel_peers[i])) for i in range(7)
    ]

    inputs = [
        pltpu.make_async_copy(src, dst, input_sem.at[i])
        for i, (src, dst) in enumerate(
            (
                (list_hbm, list_ref),
                (area_hbm, area_ref),
                (volume_hbm, volume_ref),
                (nbr_hbm, nbr_ref),
                (type_hbm, type_ref),
                (stream_hbm, stream_ref),
            )
        )
    ]
    inputs[0].start()
    load(0).start()
    for copy in inputs[1:]:
        copy.start()
    for c in range(1, CHUNKS):
        load(c).start()

    inputs[0].wait()
    send_picks[...] = one_hot(
        CELLS, 0, jnp.concatenate([list_ref[d : d + 1, :] for d in range(4)], axis=1)
    )

    def pack(c):
        rows = pl.ds(pl.multiple_of(c * CHUNK, CHUNK), CHUNK)
        high, low = two_parts(dist_v[rows, :])
        parts[c, 0:CHUNK, :] = high
        parts[c, CHUNK : 2 * CHUNK, :] = low
        both = jnp.dot(parts[c], send_picks[...], preferred_element_type=F32)
        picked = both[0:CHUNK] + both[CHUNK : 2 * CHUNK]
        for d in range(4):
            outgoing[d, rows, :] = picked[:, d * SEND : (d + 1) * SEND]

    def start_sends(c):
        for d in (2, 3, 0, 1):
            send(c, d).start()

    load(0).wait()
    pack(0)
    pl.semaphore_wait(barrier, len(greeted))
    start_sends(0)
    for copy in inputs[1:]:
        copy.wait()
    normal[...] = jnp.zeros_like(normal)
    for k in range(6):
        for axis in range(3):
            normal[axis, k : k + 1, :] = area_ref[3 * k + axis : 3 * k + axis + 1, :]
    areas = jnp.sqrt(normal[0] * normal[0] + normal[1] * normal[1] + normal[2] * normal[2])
    volume = volume_ref[...].reshape(1, CELLS)
    limit = volume / (TOP_SPEED * jnp.sum(areas, axis=0, keepdims=True))
    lowest = jnp.minimum(
        jnp.minimum(limit[:, 0:128], limit[:, 128:256]),
        jnp.minimum(limit[:, 256:384], limit[:, 384:512]),
    )
    min_msg[...] = lowest
    for copy in near_copies:
        copy.start()

    def pack_and_send(c, _):
        load(c).wait()
        pack(c)
        start_sends(c)
        return 0

    lax.fori_loop(1, FIRST, pack_and_send, 0)

    def pack_rest(c, _):
        load(c).wait()
        pack(c)
        return 0

    lax.fori_loop(FIRST, CHUNKS, pack_rest, 0)

    speed = lax.broadcasted_iota(jnp.int32, (NODES, CELLS), 0).astype(F32) - HALF
    for k in range(6):
        slope[k] = speed * normal[2, k : k + 1, :]
    for axis in range(3):
        normal[axis, 6:7, :] = jnp.sum(normal[axis, 0:6, :], axis=0, keepdims=True)
    slope[6] = speed * normal[2, 6:7, :]
    kind = type_ref[...]
    cell_ids = lax.broadcasted_iota(jnp.int32, (6, CELLS), 1)
    source[0:6, :] = jnp.where(kind == 0, nbr_ref[...], jnp.where(kind == 2, cell_ids, -1))
    inflow[0:6, :] = jnp.where(kind == 1, 1.0, 0.0)

    for i in range(14):
        start = min(i * 128, VELS - 128)
        row = stream_ref[start : start + 128].reshape(1, 128)
        stream_b[start : start + 128, :] = jnp.broadcast_to(row, (128, 128)).T

    def fill(i, _):
        k = i // 8
        base = (i % 8) * 128
        picks[k, pl.ds(pl.multiple_of(base, 128), 128), :] = one_hot(
            128, base, source[pl.ds(k, 1), :]
        )
        return 0

    lax.fori_loop(0, 48, fill, 0)

    sums[...] = jnp.zeros_like(sums)

    def old_moments(group, _):
        rows = pl.ds(pl.multiple_of(group * NODES, NODES), NODES)
        cx, cy = group_speeds(v, group)
        d = dist_v[rows, :]
        d1 = d * speed
        d2 = d1 * speed
        d3 = d2 * speed
        s0, s1, s2, s3 = fold(d), fold(d1), fold(d2), fold(d3)
        sq = cx * cx + cy * cy
        r0 = sq * s0 + s2
        terms = (
            s0,
            cx * s0,
            cy * s0,
            s1,
            (cx * cx) * s0,
            (cy * cy) * s0,
            s2,
            (cx * cy) * s0,
            cx * s1,
            cy * s1,
            cx * r0,
            cy * r0,
            sq * s1 + s3,
        )
        for i, term in enumerate(terms):
            sums[i] += term
        return 0

    lax.fori_loop(0, VELS // NODES, old_moments, 0)
    old_msg[...] = jnp.zeros_like(old_msg)
    for i in range(13):
        old_msg[i : i + 1, :] = jnp.sum(sums[i], axis=0, keepdims=True)
    for copy in near_copies:
        copy.wait()
    lowest = min_msg[...]
    for i in range(near - 1):
        lowest = jnp.minimum(lowest, min_in[i])
    min_msg2[...] = lowest
    for copy in far_copies:
        copy.start()
    for copy in x_copies:
        copy.start()

    def send_next(c, _):
        start_sends(c)
        return 0

    lax.fori_loop(FIRST, WINDOW, send_next, 0)
    def products(lhs, first, last):
        for k in range(6):
            gathered[k] = jnp.dot(
                lhs, picks[k, first:last, :], preferred_element_type=F32
            )

    def picked_rows(k, g):
        one = pl.ds(pl.multiple_of(g * NODES, NODES), NODES)
        two = pl.ds(pl.multiple_of(CHUNK + g * NODES, NODES), NODES)
        return gathered[k, one, :] + gathered[k, two, :]

    def normal_speed(k, cx, cy):
        return (cx * normal[0, k : k + 1, :] + cy * normal[1, k : k + 1, :]) + slope[k]

    def flux(c, local, remote):
        if remote:
            arrived_rows = pl.ds(pl.multiple_of(c * CHUNK, CHUNK), CHUNK)
            for d in range(4):
                high, low = two_parts(arrived[d, arrived_rows, :])
                lanes = slice(d * SEND, (d + 1) * SEND)
                arrived_parts[0:CHUNK, lanes] = high
                arrived_parts[CHUNK : 2 * CHUNK, lanes] = low
        if local and remote:
            products(jnp.concatenate([parts[c], arrived_parts[...]], axis=1), 0, 2 * CELLS)
        elif local:
            products(parts[c], 0, CELLS)
        else:
            products(arrived_parts[...], CELLS, 2 * CELLS)

        def one_group(g, _):
            group = c * GROUPS + g
            rows = pl.ds(pl.multiple_of(group * NODES, NODES), NODES)
            cx, cy = group_speeds(v, group)
            inward = jnp.zeros((NODES, CELLS), F32)
            free = jnp.zeros((NODES, CELLS), F32)
            total = jnp.zeros((NODES, CELLS), F32)
            for k in range(6):
                u = jnp.minimum(normal_speed(k, cx, cy), 0.0)
                total += u * picked_rows(k, g)
                if local:
                    inward += u
                    free += u * inflow[k : k + 1, :]
            if local:
                stream = stream_b[rows, :]
                stream = jnp.concatenate([stream] * 4, axis=1)
                outward = normal_speed(6, cx, cy) - inward
                total += outward * dist_v[rows, :] + free * stream
            else:
                total += moved[rows, :]
            moved[rows, :] = total
            if remote:
                t1 = total * speed
                s0, s1, s2 = fold(total), fold(t1), fold(t1 * speed)
                sums[0] += s0
                sums[1] += cx * s0
                sums[2] += cy * s0
                sums[3] += s1
                sums[4] += 0.5 * ((cx * cx + cy * cy) * s0 + s2)
            return 0

        lax.fori_loop(0, GROUPS, one_group, 0)

    def local_part(c, _):
        flux(c, True, False)
        return 0

    lax.fori_loop(SPLIT, CHUNKS, local_part, 0)
    for i in range(5):
        sums[i] = jnp.zeros((8, CELLS), F32)

    def arrive(c):
        for d in range(4):
            send(c, d).wait_recv()

        @pl.when(c + WINDOW < CHUNKS)
        def _():
            for d in range(4):
                send(c, d).wait_send()
            start_sends(c + WINDOW)

    def whole_part(c, _):
        arrive(c)

        @pl.when(c == 4)
        def _():
            for copy in x_copies:
                copy.wait()
            old_msg2[...] = old_msg[...] + old_in[0] + old_in[1] + old_in[2]
            z_copy.start()

        flux(c, True, True)
        return 0

    lax.fori_loop(0, SPLIT, whole_part, 0)

    def remote_part(c, _):
        arrive(c)
        flux(c, False, True)
        return 0

    lax.fori_loop(SPLIT, CHUNKS, remote_part, 0)

    new_msg[...] = jnp.zeros_like(new_msg)
    for i in range(5):
        row = jnp.sum(sums[i], axis=0, keepdims=True)
        for t in range(4):
            new_msg[4 * i + t : 4 * i + t + 1, :] = row[:, 128 * t : 128 * t + 128]
    for copy in new_copies:
        copy.start()

    for copy in far_copies:
        copy.wait()
    lowest = min_msg2[...]
    for i in range(far - 1):
        lowest = jnp.minimum(lowest, min_in2[i])
    time_step = CFL * jnp.min(lowest, axis=1, keepdims=True)
    time_step = jnp.broadcast_to(time_step, (1, CELLS))
    z_copy.wait()
    old = old_msg2[...] + old_in2[...]
    rho = old[0:1]
    mean = [old[1 + i : 2 + i] / rho for i in range(3)]
    pressure = [[old[4:5], old[7:8], old[8:9]], [old[7:8], old[5:6], old[9:10]], [old[8:9], old[9:10], old[6:7]]]
    trace = old[4:5] + old[5:6] + old[6:7]
    mean_sq = mean[0] * mean[0] + mean[1] * mean[1] + mean[2] * mean[2]
    for i in range(3):
        along = (
            mean[0] * pressure[i][0] + mean[1] * pressure[i][1] + mean[2] * pressure[i][2]
        )
        coef_ref[8 + i : 9 + i, :] = 0.5 * (
            old[10 + i : 11 + i] - 2.0 * along - mean[i] * trace + 2.0 * rho * mean_sq * mean[i]
        )
    ratio = time_step / volume
    coef_ref[5:6, :] = ratio
    coef_ref[6:7, :] = time_step
    coef_ref[7:8, :] = jnp.zeros((1, CELLS), F32)
    coef_ref[11:16, :] = jnp.zeros((5, CELLS), F32)

    def finish_sends(c, _):
        for d in range(4):
            send(c, d).wait_send()
        return 0

    lax.fori_loop(CHUNKS - WINDOW, CHUNKS, finish_sends, 0)
    for copy in new_copies:
        copy.wait()
    total = new_msg[...]
    for i in range(7):
        total = total + new_in[i]
    energy = 0.5 * trace
    for i in range(5):
        phi = jnp.concatenate([total[4 * i + t : 4 * i + t + 1] for t in range(4)], axis=1)
        before = energy if i == 4 else old[i : i + 1]
        coef_ref[i : i + 1, :] = before - ratio * phi


def relax(dist_v, moved, coef_ref, out_hbm, result, first, second, third, sem):
    v = lax.axis_index("vel")
    rho = coef_ref[0:1, :]
    mean = [coef_ref[1 + i : 2 + i, :] / rho for i in range(3)]
    heat = [coef_ref[8 + i : 9 + i, :] for i in range(3)]
    ratio = coef_ref[5:6, :]
    time_step = coef_ref[6:7, :]
    mean_sq = mean[0] * mean[0] + mean[1] * mean[1] + mean[2] * mean[2]
    temp = (2.0 * coef_ref[4:5, :] / rho - mean_sq) / 3.0
    relax_time = MU_REF * jnp.exp(OMEGA * jnp.log(temp)) / (rho * temp)
    relax_ratio = time_step / relax_time
    keep = 1.0 / (1.0 + relax_ratio)
    cold = 1.0 / temp
    root = lax.rsqrt(2.0 * math.pi * temp)
    scale = relax_ratio * keep * rho * (root * root * root)
    bend = (1.0 - PRANDTL) / (5.0 * rho * temp * temp)
    speed = lax.broadcasted_iota(jnp.int32, (NODES, CELLS), 0).astype(F32) - HALF
    for axis, table in ((1, second), (2, third)):
        rel = speed - mean[axis]
        sq = rel * rel * cold
        table[0] = jnp.exp(-0.5 * sq)
        table[1] = sq
        table[2] = rel * (heat[axis] * bend)
    own = lax.broadcasted_iota(jnp.int32, (8, CELLS), 0).astype(F32) - HALF
    rel = own + (v * 3).astype(F32) - mean[0]
    sq = rel * rel * cold
    first[0] = jnp.exp(-0.5 * sq) * scale
    first[1] = sq - 5.0
    first[2] = rel * (heat[0] * bend)

    def one_chunk(c, _):
        def one_group(g, _):
            group = c * GROUPS + g
            rows = pl.ds(pl.multiple_of(group * NODES, NODES), NODES)
            a = pl.ds(group // NODES, 1)
            b = pl.ds(group % NODES, 1)
            weight = first[0, a, :] * second[0, b, :]
            sq = (first[1, a, :] + second[1, b, :]) + third[1]
            along = (first[2, a, :] + second[2, b, :]) + third[2]
            gauss = weight * third[0]
            rest = dist_v[rows, :] - ratio * moved[rows, :]
            result[rows, :] = rest * keep + gauss * (1.0 + along * sq)
            return 0

        lax.fori_loop(0, GROUPS, one_group, 0)
        rows = pl.ds(pl.multiple_of(c * CHUNK, CHUNK), CHUNK)
        pltpu.make_async_copy(result.at[rows], out_hbm.at[rows], sem.at[c]).start()
        return 0

    lax.fori_loop(0, CHUNKS, one_chunk, 0)

    def finish(c, _):
        rows = pl.ds(pl.multiple_of(c * CHUNK, CHUNK), CHUNK)
        pltpu.make_async_copy(result.at[rows], out_hbm.at[rows], sem.at[c]).wait()
        return 0

    lax.fori_loop(0, CHUNKS, finish, 0)


def solution(mesh):
    n_space = mesh.shape["space"]
    vmem = pl.BlockSpec(memory_space=pltpu.VMEM)
    hbm = pl.BlockSpec(memory_space=pl.ANY)
    raw = pl.BlockSpec(memory_space=pltpu.HBM)

    def local(dist, free_stream, area_normal, cell_volume, face_nbr, face_type, send_list):
        own, moved, coef = pl.pallas_call(
            functools.partial(transport, n_space),
            out_shape=(
                jax.ShapeDtypeStruct((VELS, CELLS), F32),
                jax.ShapeDtypeStruct((VELS, CELLS), F32),
                jax.ShapeDtypeStruct((16, CELLS), F32),
            ),
            in_specs=[raw] * 7,
            out_specs=(vmem, vmem, vmem),
            scratch_shapes=[
                pltpu.VMEM((VELS,), F32),
                pltpu.VMEM((18, CELLS), F32),
                pltpu.VMEM((CELLS,), F32),
                pltpu.VMEM((6, CELLS), jnp.int32),
                pltpu.VMEM((6, CELLS), jnp.int32),
                pltpu.VMEM((4, SEND), jnp.int32),
                pltpu.VMEM((CHUNKS, 2 * CHUNK, CELLS), BF16),
                pltpu.VMEM((4, VELS, SEND), F32),
                pltpu.VMEM((4, VELS, SEND), F32),
                pltpu.VMEM((6, 2 * CELLS, CELLS), BF16),
                pltpu.VMEM((CELLS, CELLS), BF16),
                pltpu.VMEM((6, 2 * CHUNK, CELLS), F32),
                pltpu.VMEM((2 * CHUNK, CELLS), BF16),
                pltpu.VMEM((3, 8, CELLS), F32),
                pltpu.VMEM((7, NODES, CELLS), F32),
                pltpu.VMEM((8, CELLS), F32),
                pltpu.VMEM((8, CELLS), jnp.int32),
                pltpu.VMEM((VELS, 128), F32),
                pltpu.VMEM((13, 8, CELLS), F32),
                pltpu.VMEM((16, CELLS), F32),
                pltpu.VMEM((3, 16, CELLS), F32),
                pltpu.VMEM((16, CELLS), F32),
                pltpu.VMEM((16, CELLS), F32),
                pltpu.VMEM((24, 128), F32),
                pltpu.VMEM((7, 24, 128), F32),
                pltpu.VMEM((1, 128), F32),
                pltpu.VMEM((7, 1, 128), F32),
                pltpu.VMEM((1, 128), F32),
                pltpu.VMEM((n_space // 8 - 1, 1, 128), F32),
                pltpu.SemaphoreType.DMA((CHUNKS,)),
                pltpu.SemaphoreType.DMA((6,)),
                pltpu.SemaphoreType.DMA((CHUNKS, 4)),
                pltpu.SemaphoreType.DMA((CHUNKS, 4)),
                pltpu.SemaphoreType.DMA((21,)),
                pltpu.SemaphoreType.DMA((21,)),
            ],
            compiler_params=pltpu.CompilerParams(
                collective_id=0, has_side_effects=True, vmem_limit_bytes=44 * 2**20
            ),
            name="transport",
        )(
            *[
                pltpu.with_memory_space_constraint(x, pltpu.HBM)
                for x in (
                    dist,
                    free_stream,
                    area_normal,
                    cell_volume,
                    face_nbr,
                    face_type,
                    send_list,
                )
            ]
        )
        return pl.pallas_call(
            relax,
            out_shape=jax.ShapeDtypeStruct((VELS, CELLS), F32),
            in_specs=[vmem] * 3,
            out_specs=hbm,
            scratch_shapes=[
                pltpu.VMEM((VELS, CELLS), F32),
                pltpu.VMEM((3, 8, CELLS), F32),
                pltpu.VMEM((3, NODES, CELLS), F32),
                pltpu.VMEM((3, NODES, CELLS), F32),
                pltpu.SemaphoreType.DMA((CHUNKS,)),
            ],
            compiler_params=pltpu.CompilerParams(vmem_limit_bytes=24 * 2**20),
            name="relax",
        )(own, moved, coef)

    return jax.shard_map(
        local,
        mesh=mesh,
        in_specs=(
            P("vel", "space"),
            P("vel"),
            P(None, "space"),
            P("space"),
            P(None, "space"),
            P(None, "space"),
            P(None, "space"),
        ),
        out_specs=P("vel", "space"),
        check_vma=False,
    )
```

```python
import functools
import math

import jax
import jax.numpy as jnp
from jax import lax
from jax.experimental import pallas as pl
from jax.experimental.pallas import tpu as pltpu
from jax.sharding import PartitionSpec as P

MESH = pl.DeviceIdType.MESH
F32 = jnp.float32
BF16 = jnp.bfloat16

NODES = 24
HALF = (NODES - 1) / 2.0
TOP_SPEED = HALF * math.sqrt(3.0)
CFL = 0.9
MU_REF = 60.0
OMEGA = 0.81
PRANDTL = 2.0 / 3.0
STEPS = (1, -1, 2, -2)

VELS = 1728
CELLS = 512
SEND = 128
CHUNK = 144
CHUNKS = VELS // CHUNK
GROUPS = CHUNK // NODES
FIRST = 3
SPLIT = 6


def two_parts(x):
    high = x.astype(BF16)
    low = (x - high.astype(F32)).astype(BF16)
    return high, low


def fold(x):
    return x[0:8] + x[8:16] + x[16:24]


def group_speeds(vel, group):
    first = (vel * 3 + group // NODES).astype(F32) - HALF
    second = (group % NODES).astype(F32) - HALF
    return first, second


def one_hot(rows, base, wanted):
    ids = lax.broadcasted_iota(jnp.int32, (rows, wanted.shape[1]), 0) + base
    return jnp.where(ids == wanted, 1.0, 0.0).astype(BF16)


def transport(
    n_space,
    dist_hbm,
    stream_hbm,
    area_hbm,
    volume_hbm,
    nbr_hbm,
    type_hbm,
    list_hbm,
    dist_v,
    moved,
    coef_ref,
    stream_ref,
    area_ref,
    volume_ref,
    nbr_ref,
    type_ref,
    list_ref,
    parts,
    outgoing,
    arrived,
    picks,
    send_picks,
    gathered,
    arrived_parts,
    normal,
    slope,
    inflow,
    source,
    stream_b,
    sums,
    old_msg,
    old_in,
    old_msg2,
    old_in2,
    new_msg,
    new_in,
    min_msg,
    min_in,
    min_msg2,
    min_in2,
    load_sem,
    input_sem,
    send_sem,
    recv_sem,
    small_send,
    small_recv,
):
    s = lax.axis_index("space")
    v = lax.axis_index("vel")
    near = 8
    far = n_space // near
    partners = [lax.rem(s + step + n_space, n_space) for step in STEPS]
    near_peers = [(s // near) * near + lax.rem(s + i, near) for i in range(1, near)]
    far_peers = [lax.rem(s + near * i, n_space) for i in range(1, far)]
    vel_peers = [lax.rem(v + i, 8) for i in (4, 5, 3, 6, 2, 7, 1)]
    x_peers = [lax.rem(v + 2 * i, 8) for i in range(1, 4)]
    z_peer = v + 1 - 2 * lax.rem(v, 2)

    barrier = pltpu.get_barrier_semaphore()
    greeted = [(q, v) for q in partners + near_peers + far_peers]
    greeted += [(s, q) for q in vel_peers]
    for q in greeted:
        pl.semaphore_signal(barrier, inc=1, device_id=q, device_id_type=MESH)

    def load(c):
        rows = pl.ds(pl.multiple_of(c * CHUNK, CHUNK), CHUNK)
        return pltpu.make_async_copy(dist_hbm.at[rows], dist_v.at[rows], load_sem.at[c])

    def send(c, d):
        rows = pl.ds(pl.multiple_of(c * CHUNK, CHUNK), CHUNK)
        return pltpu.make_async_remote_copy(
            src_ref=outgoing.at[d, rows],
            dst_ref=arrived.at[d, rows],
            send_sem=send_sem.at[c, d],
            recv_sem=recv_sem.at[c, d],
            device_id=(partners[d], v),
            device_id_type=MESH,
        )

    def small(src, dst, at, where):
        return pltpu.make_async_remote_copy(
            src_ref=src,
            dst_ref=dst,
            send_sem=small_send.at[at],
            recv_sem=small_recv.at[at],
            device_id=where,
            device_id_type=MESH,
        )

    near_copies = [
        small(min_msg, min_in.at[i], i, (near_peers[i], v)) for i in range(near - 1)
    ]
    far_copies = [
        small(min_msg2, min_in2.at[i], 7 + i, (far_peers[i], v)) for i in range(far - 1)
    ]
    x_copies = [small(old_msg, old_in.at[i], 10 + i, (s, x_peers[i])) for i in range(3)]
    z_copy = small(old_msg2, old_in2, 13, (s, z_peer))
    new_copies = [
        small(new_msg, new_in.at[i], 14 + i, (s, vel_peers[i])) for i in range(7)
    ]

    inputs = [
        pltpu.make_async_copy(src, dst, input_sem.at[i])
        for i, (src, dst) in enumerate(
            (
                (list_hbm, list_ref),
                (area_hbm, area_ref),
                (volume_hbm, volume_ref),
                (nbr_hbm, nbr_ref),
                (type_hbm, type_ref),
                (stream_hbm, stream_ref),
            )
        )
    ]
    inputs[0].start()
    load(0).start()
    for copy in inputs[1:]:
        copy.start()
    for c in range(1, CHUNKS):
        load(c).start()

    inputs[0].wait()
    send_picks[...] = one_hot(
        CELLS, 0, jnp.concatenate([list_ref[d : d + 1, :] for d in range(4)], axis=1)
    )

    def pack(c):
        rows = pl.ds(pl.multiple_of(c * CHUNK, CHUNK), CHUNK)
        high, low = two_parts(dist_v[rows, :])
        parts[c, 0:CHUNK, :] = high
        parts[c, CHUNK : 2 * CHUNK, :] = low
        both = jnp.dot(parts[c], send_picks[...], preferred_element_type=F32)
        picked = both[0:CHUNK] + both[CHUNK : 2 * CHUNK]
        for d in range(4):
            outgoing[d, rows, :] = picked[:, d * SEND : (d + 1) * SEND]

    def start_sends(c):
        for d in (2, 3, 0, 1):
            send(c, d).start()

    load(0).wait()
    pack(0)
    pl.semaphore_wait(barrier, len(greeted))
    start_sends(0)
    for copy in inputs[1:]:
        copy.wait()
    normal[...] = jnp.zeros_like(normal)
    for k in range(6):
        for axis in range(3):
            normal[axis, k : k + 1, :] = area_ref[3 * k + axis : 3 * k + axis + 1, :]
    areas = jnp.sqrt(normal[0] * normal[0] + normal[1] * normal[1] + normal[2] * normal[2])
    volume = volume_ref[...].reshape(1, CELLS)
    limit = volume / (TOP_SPEED * jnp.sum(areas, axis=0, keepdims=True))
    lowest = jnp.minimum(
        jnp.minimum(limit[:, 0:128], limit[:, 128:256]),
        jnp.minimum(limit[:, 256:384], limit[:, 384:512]),
    )
    min_msg[...] = lowest
    for copy in near_copies:
        copy.start()

    def pack_and_send(c, _):
        load(c).wait()
        pack(c)
        start_sends(c)
        return 0

    lax.fori_loop(1, FIRST, pack_and_send, 0)

    def pack_rest(c, _):
        load(c).wait()
        pack(c)
        return 0

    lax.fori_loop(FIRST, CHUNKS, pack_rest, 0)

    speed = lax.broadcasted_iota(jnp.int32, (NODES, CELLS), 0).astype(F32) - HALF
    for k in range(6):
        slope[k] = speed * normal[2, k : k + 1, :]
    for axis in range(3):
        normal[axis, 6:7, :] = jnp.sum(normal[axis, 0:6, :], axis=0, keepdims=True)
    slope[6] = speed * normal[2, 6:7, :]
    kind = type_ref[...]
    cell_ids = lax.broadcasted_iota(jnp.int32, (6, CELLS), 1)
    source[0:6, :] = jnp.where(kind == 0, nbr_ref[...], jnp.where(kind == 2, cell_ids, -1))
    inflow[0:6, :] = jnp.where(kind == 1, 1.0, 0.0)

    for i in range(14):
        start = min(i * 128, VELS - 128)
        row = stream_ref[start : start + 128].reshape(1, 128)
        stream_b[start : start + 128, :] = jnp.broadcast_to(row, (128, 128)).T

    def fill(i, _):
        k = i // 8
        base = (i % 8) * 128
        picks[k, pl.ds(pl.multiple_of(base, 128), 128), :] = one_hot(
            128, base, source[pl.ds(k, 1), :]
        )
        return 0

    lax.fori_loop(0, 48, fill, 0)

    sums[...] = jnp.zeros_like(sums)

    def old_moments(group, _):
        rows = pl.ds(pl.multiple_of(group * NODES, NODES), NODES)
        cx, cy = group_speeds(v, group)
        d = dist_v[rows, :]
        d1 = d * speed
        d2 = d1 * speed
        d3 = d2 * speed
        s0, s1, s2, s3 = fold(d), fold(d1), fold(d2), fold(d3)
        sq = cx * cx + cy * cy
        r0 = sq * s0 + s2
        terms = (
            s0,
            cx * s0,
            cy * s0,
            s1,
            (cx * cx) * s0,
            (cy * cy) * s0,
            s2,
            (cx * cy) * s0,
            cx * s1,
            cy * s1,
            cx * r0,
            cy * r0,
            sq * s1 + s3,
        )
        for i, term in enumerate(terms):
            sums[i] += term
        return 0

    lax.fori_loop(0, VELS // NODES, old_moments, 0)
    old_msg[...] = jnp.zeros_like(old_msg)
    for i in range(13):
        old_msg[i : i + 1, :] = jnp.sum(sums[i], axis=0, keepdims=True)
    for copy in near_copies:
        copy.wait()
    lowest = min_msg[...]
    for i in range(near - 1):
        lowest = jnp.minimum(lowest, min_in[i])
    min_msg2[...] = lowest
    for copy in far_copies:
        copy.start()
    for copy in x_copies:
        copy.start()

    def send_next(c, _):
        start_sends(c)
        return 0

    lax.fori_loop(FIRST, CHUNKS, send_next, 0)
    def products(lhs, first, last):
        for k in range(6):
            gathered[k] = jnp.dot(
                lhs, picks[k, first:last, :], preferred_element_type=F32
            )

    def picked_rows(k, g):
        one = pl.ds(pl.multiple_of(g * NODES, NODES), NODES)
        two = pl.ds(pl.multiple_of(CHUNK + g * NODES, NODES), NODES)
        return gathered[k, one, :] + gathered[k, two, :]

    def normal_speed(k, cx, cy):
        return (cx * normal[0, k : k + 1, :] + cy * normal[1, k : k + 1, :]) + slope[k]

    def flux(c, local, remote):
        if remote:
            arrived_rows = pl.ds(pl.multiple_of(c * CHUNK, CHUNK), CHUNK)
            for d in range(4):
                high, low = two_parts(arrived[d, arrived_rows, :])
                lanes = slice(d * SEND, (d + 1) * SEND)
                arrived_parts[0:CHUNK, lanes] = high
                arrived_parts[CHUNK : 2 * CHUNK, lanes] = low
        if local and remote:
            products(jnp.concatenate([parts[c], arrived_parts[...]], axis=1), 0, 2 * CELLS)
        elif local:
            products(parts[c], 0, CELLS)
        else:
            products(arrived_parts[...], CELLS, 2 * CELLS)

        def one_group(g, _):
            group = c * GROUPS + g
            rows = pl.ds(pl.multiple_of(group * NODES, NODES), NODES)
            cx, cy = group_speeds(v, group)
            inward = jnp.zeros((NODES, CELLS), F32)
            free = jnp.zeros((NODES, CELLS), F32)
            total = jnp.zeros((NODES, CELLS), F32)
            for k in range(6):
                u = jnp.minimum(normal_speed(k, cx, cy), 0.0)
                total += u * picked_rows(k, g)
                if local:
                    inward += u
                    free += u * inflow[k : k + 1, :]
            if local:
                stream = stream_b[rows, :]
                stream = jnp.concatenate([stream] * 4, axis=1)
                outward = normal_speed(6, cx, cy) - inward
                total += outward * dist_v[rows, :] + free * stream
            else:
                total += moved[rows, :]
            moved[rows, :] = total
            if remote:
                t1 = total * speed
                s0, s1, s2 = fold(total), fold(t1), fold(t1 * speed)
                sums[0] += s0
                sums[1] += cx * s0
                sums[2] += cy * s0
                sums[3] += s1
                sums[4] += 0.5 * ((cx * cx + cy * cy) * s0 + s2)
            return 0

        lax.fori_loop(0, GROUPS, one_group, 0, unroll=2)

    def local_part(c, _):
        flux(c, True, False)
        return 0

    lax.fori_loop(SPLIT, CHUNKS, local_part, 0)
    for i in range(5):
        sums[i] = jnp.zeros((8, CELLS), F32)

    def arrive(c):
        for d in range(4):
            send(c, d).wait_recv()

    def whole_part(c, _):
        arrive(c)

        @pl.when(c == 4)
        def _():
            for copy in x_copies:
                copy.wait()
            old_msg2[...] = old_msg[...] + old_in[0] + old_in[1] + old_in[2]
            z_copy.start()

        flux(c, True, True)
        return 0

    lax.fori_loop(0, SPLIT, whole_part, 0)

    def finish_sends(c, _):
        for d in range(4):
            send(c, d).wait_send()
        return 0

    def remote_part(c, _):
        arrive(c)
        flux(c, False, True)
        finish_sends(c - SPLIT, 0)
        return 0

    lax.fori_loop(SPLIT, CHUNKS, remote_part, 0)

    new_msg[...] = jnp.zeros_like(new_msg)
    for i in range(5):
        row = jnp.sum(sums[i], axis=0, keepdims=True)
        for t in range(4):
            new_msg[4 * i + t : 4 * i + t + 1, :] = row[:, 128 * t : 128 * t + 128]
    for copy in new_copies:
        copy.start()

    for copy in far_copies:
        copy.wait()
    lowest = min_msg2[...]
    for i in range(far - 1):
        lowest = jnp.minimum(lowest, min_in2[i])
    time_step = CFL * jnp.min(lowest, axis=1, keepdims=True)
    time_step = jnp.broadcast_to(time_step, (1, CELLS))
    z_copy.wait()
    old = old_msg2[...] + old_in2[...]
    rho = old[0:1]
    mean = [old[1 + i : 2 + i] / rho for i in range(3)]
    pressure = [[old[4:5], old[7:8], old[8:9]], [old[7:8], old[5:6], old[9:10]], [old[8:9], old[9:10], old[6:7]]]
    trace = old[4:5] + old[5:6] + old[6:7]
    mean_sq = mean[0] * mean[0] + mean[1] * mean[1] + mean[2] * mean[2]
    for i in range(3):
        along = (
            mean[0] * pressure[i][0] + mean[1] * pressure[i][1] + mean[2] * pressure[i][2]
        )
        coef_ref[8 + i : 9 + i, :] = 0.5 * (
            old[10 + i : 11 + i] - 2.0 * along - mean[i] * trace + 2.0 * rho * mean_sq * mean[i]
        )
    ratio = time_step / volume
    coef_ref[5:6, :] = ratio
    coef_ref[6:7, :] = time_step
    coef_ref[7:8, :] = jnp.zeros((1, CELLS), F32)
    coef_ref[11:16, :] = jnp.zeros((5, CELLS), F32)

    lax.fori_loop(CHUNKS - SPLIT, CHUNKS, finish_sends, 0)
    total = new_msg[...]
    for i in range(7):
        new_copies[i].wait_recv()
        total = total + new_in[i]
    for copy in new_copies:
        copy.wait_send()
    energy = 0.5 * trace
    for i in range(5):
        phi = jnp.concatenate([total[4 * i + t : 4 * i + t + 1] for t in range(4)], axis=1)
        before = energy if i == 4 else old[i : i + 1]
        coef_ref[i : i + 1, :] = before - ratio * phi


def relax(dist_v, moved, coef_ref, out_hbm, result, first, second, third, sem):
    v = lax.axis_index("vel")
    rho = coef_ref[0:1, :]
    mean = [coef_ref[1 + i : 2 + i, :] / rho for i in range(3)]
    heat = [coef_ref[8 + i : 9 + i, :] for i in range(3)]
    ratio = coef_ref[5:6, :]
    time_step = coef_ref[6:7, :]
    mean_sq = mean[0] * mean[0] + mean[1] * mean[1] + mean[2] * mean[2]
    temp = (2.0 * coef_ref[4:5, :] / rho - mean_sq) / 3.0
    relax_time = MU_REF * jnp.exp(OMEGA * jnp.log(temp)) / (rho * temp)
    relax_ratio = time_step / relax_time
    keep = 1.0 / (1.0 + relax_ratio)
    cold = 1.0 / temp
    root = lax.rsqrt(2.0 * math.pi * temp)
    scale = relax_ratio * keep * rho * (root * root * root)
    bend = (1.0 - PRANDTL) / (5.0 * rho * temp * temp)
    speed = lax.broadcasted_iota(jnp.int32, (NODES, CELLS), 0).astype(F32) - HALF
    for axis, table in ((1, second), (2, third)):
        rel = speed - mean[axis]
        sq = rel * rel * cold
        table[0] = jnp.exp(-0.5 * sq)
        table[1] = sq
        table[2] = rel * (heat[axis] * bend)
    own = lax.broadcasted_iota(jnp.int32, (8, CELLS), 0).astype(F32) - HALF
    rel = own + (v * 3).astype(F32) - mean[0]
    sq = rel * rel * cold
    first[0] = jnp.exp(-0.5 * sq) * scale
    first[1] = sq - 5.0
    first[2] = rel * (heat[0] * bend)

    def one_chunk(c, _):
        def one_group(g, _):
            group = c * GROUPS + g
            rows = pl.ds(pl.multiple_of(group * NODES, NODES), NODES)
            a = pl.ds(group // NODES, 1)
            b = pl.ds(group % NODES, 1)
            weight = first[0, a, :] * second[0, b, :]
            sq = (first[1, a, :] + second[1, b, :]) + third[1]
            along = (first[2, a, :] + second[2, b, :]) + third[2]
            gauss = weight * third[0]
            rest = dist_v[rows, :] - ratio * moved[rows, :]
            result[rows, :] = rest * keep + gauss * (1.0 + along * sq)
            return 0

        lax.fori_loop(0, GROUPS, one_group, 0, unroll=True)
        rows = pl.ds(pl.multiple_of(c * CHUNK, CHUNK), CHUNK)
        pltpu.make_async_copy(result.at[rows], out_hbm.at[rows], sem.at[c]).start()
        return 0

    lax.fori_loop(0, CHUNKS, one_chunk, 0)

    def finish(c, _):
        rows = pl.ds(pl.multiple_of(c * CHUNK, CHUNK), CHUNK)
        pltpu.make_async_copy(result.at[rows], out_hbm.at[rows], sem.at[c]).wait()
        return 0

    lax.fori_loop(0, CHUNKS, finish, 0)


def solution(mesh):
    n_space = mesh.shape["space"]
    vmem = pl.BlockSpec(memory_space=pltpu.VMEM)
    hbm = pl.BlockSpec(memory_space=pl.ANY)
    raw = pl.BlockSpec(memory_space=pltpu.HBM)

    def local(dist, free_stream, area_normal, cell_volume, face_nbr, face_type, send_list):
        own, moved, coef = pl.pallas_call(
            functools.partial(transport, n_space),
            out_shape=(
                jax.ShapeDtypeStruct((VELS, CELLS), F32),
                jax.ShapeDtypeStruct((VELS, CELLS), F32),
                jax.ShapeDtypeStruct((16, CELLS), F32),
            ),
            in_specs=[raw] * 7,
            out_specs=(vmem, vmem, vmem),
            scratch_shapes=[
                pltpu.VMEM((VELS,), F32),
                pltpu.VMEM((18, CELLS), F32),
                pltpu.VMEM((CELLS,), F32),
                pltpu.VMEM((6, CELLS), jnp.int32),
                pltpu.VMEM((6, CELLS), jnp.int32),
                pltpu.VMEM((4, SEND), jnp.int32),
                pltpu.VMEM((CHUNKS, 2 * CHUNK, CELLS), BF16),
                pltpu.VMEM((4, VELS, SEND), F32),
                pltpu.VMEM((4, VELS, SEND), F32),
                pltpu.VMEM((6, 2 * CELLS, CELLS), BF16),
                pltpu.VMEM((CELLS, CELLS), BF16),
                pltpu.VMEM((6, 2 * CHUNK, CELLS), F32),
                pltpu.VMEM((2 * CHUNK, CELLS), BF16),
                pltpu.VMEM((3, 8, CELLS), F32),
                pltpu.VMEM((7, NODES, CELLS), F32),
                pltpu.VMEM((8, CELLS), F32),
                pltpu.VMEM((8, CELLS), jnp.int32),
                pltpu.VMEM((VELS, 128), F32),
                pltpu.VMEM((13, 8, CELLS), F32),
                pltpu.VMEM((16, CELLS), F32),
                pltpu.VMEM((3, 16, CELLS), F32),
                pltpu.VMEM((16, CELLS), F32),
                pltpu.VMEM((16, CELLS), F32),
                pltpu.VMEM((24, 128), F32),
                pltpu.VMEM((7, 24, 128), F32),
                pltpu.VMEM((1, 128), F32),
                pltpu.VMEM((7, 1, 128), F32),
                pltpu.VMEM((1, 128), F32),
                pltpu.VMEM((n_space // 8 - 1, 1, 128), F32),
                pltpu.SemaphoreType.DMA((CHUNKS,)),
                pltpu.SemaphoreType.DMA((6,)),
                pltpu.SemaphoreType.DMA((CHUNKS, 4)),
                pltpu.SemaphoreType.DMA((CHUNKS, 4)),
                pltpu.SemaphoreType.DMA((21,)),
                pltpu.SemaphoreType.DMA((21,)),
            ],
            compiler_params=pltpu.CompilerParams(
                collective_id=0, has_side_effects=True, vmem_limit_bytes=44 * 2**20
            ),
            name="transport",
        )(
            *[
                pltpu.with_memory_space_constraint(x, pltpu.HBM)
                for x in (
                    dist,
                    free_stream,
                    area_normal,
                    cell_volume,
                    face_nbr,
                    face_type,
                    send_list,
                )
            ]
        )
        return pl.pallas_call(
            relax,
            out_shape=jax.ShapeDtypeStruct((VELS, CELLS), F32),
            in_specs=[vmem] * 3,
            out_specs=hbm,
            scratch_shapes=[
                pltpu.VMEM((VELS, CELLS), F32),
                pltpu.VMEM((3, 8, CELLS), F32),
                pltpu.VMEM((3, NODES, CELLS), F32),
                pltpu.VMEM((3, NODES, CELLS), F32),
                pltpu.SemaphoreType.DMA((CHUNKS,)),
            ],
            compiler_params=pltpu.CompilerParams(vmem_limit_bytes=24 * 2**20),
            name="relax",
        )(own, moved, coef)

    return jax.shard_map(
        local,
        mesh=mesh,
        in_specs=(
            P("vel", "space"),
            P("vel"),
            P(None, "space"),
            P("space"),
            P(None, "space"),
            P(None, "space"),
            P(None, "space"),
        ),
        out_specs=P("vel", "space"),
        check_vma=False,
    )
```

```python
import functools
import math

import jax
import jax.numpy as jnp
from jax import lax
from jax.experimental import pallas as pl
from jax.experimental.pallas import tpu as pltpu
from jax.sharding import PartitionSpec as P

MESH = pl.DeviceIdType.MESH
F32 = jnp.float32
BF16 = jnp.bfloat16

NODES = 24
HALF = (NODES - 1) / 2.0
TOP_SPEED = HALF * math.sqrt(3.0)
CFL = 0.9
MU_REF = 60.0
OMEGA = 0.81
PRANDTL = 2.0 / 3.0
STEPS = (1, -1, 2, -2)

VELS = 1728
CELLS = 512
SEND = 128
CHUNK = 144
CHUNKS = VELS // CHUNK
GROUPS = CHUNK // NODES
FIRST = 3
SPLIT = 6


def two_parts(x):
    high = x.astype(BF16)
    low = (x - high.astype(F32)).astype(BF16)
    return high, low


def fold(x):
    return x[0:8] + x[8:16] + x[16:24]


def group_speeds(vel, group):
    first = (vel * 3 + group // NODES).astype(F32) - HALF
    second = (group % NODES).astype(F32) - HALF
    return first, second


def one_hot(rows, base, wanted):
    ids = lax.broadcasted_iota(jnp.int32, (rows, wanted.shape[1]), 0) + base
    return jnp.where(ids == wanted, 1.0, 0.0).astype(BF16)


def transport(
    n_space,
    dist_hbm,
    stream_hbm,
    area_hbm,
    volume_hbm,
    nbr_hbm,
    type_hbm,
    list_hbm,
    dist_v,
    moved,
    coef_ref,
    stream_ref,
    area_ref,
    volume_ref,
    nbr_ref,
    type_ref,
    list_ref,
    parts,
    outgoing,
    arrived,
    picks,
    send_picks,
    gathered,
    arrived_parts,
    normal,
    slope,
    inflow,
    source,
    stream_b,
    sums,
    old_msg,
    old_in,
    old_msg2,
    old_in2,
    new_msg,
    new_in,
    min_msg,
    min_in,
    min_msg2,
    min_in2,
    load_sem,
    input_sem,
    send_sem,
    recv_sem,
    small_send,
    small_recv,
):
    s = lax.axis_index("space")
    v = lax.axis_index("vel")
    near = 8
    far = n_space // near
    partners = [lax.rem(s + step + n_space, n_space) for step in STEPS]
    near_peers = [(s // near) * near + lax.rem(s + i, near) for i in range(1, near)]
    far_peers = [lax.rem(s + near * i, n_space) for i in range(1, far)]
    vel_peers = [lax.rem(v + i, 8) for i in (4, 5, 3, 6, 2, 7, 1)]
    x_peers = [lax.rem(v + 2 * i, 8) for i in range(1, 4)]
    z_peer = v + 1 - 2 * lax.rem(v, 2)

    barrier = pltpu.get_barrier_semaphore()
    greeted = [(q, v) for q in partners + near_peers + far_peers]
    greeted += [(s, q) for q in vel_peers]
    for q in greeted:
        pl.semaphore_signal(barrier, inc=1, device_id=q, device_id_type=MESH)

    def load(c):
        rows = pl.ds(pl.multiple_of(c * CHUNK, CHUNK), CHUNK)
        return pltpu.make_async_copy(dist_hbm.at[rows], dist_v.at[rows], load_sem.at[c])

    def send(c, d):
        rows = pl.ds(pl.multiple_of(c * CHUNK, CHUNK), CHUNK)
        return pltpu.make_async_remote_copy(
            src_ref=outgoing.at[d, rows],
            dst_ref=arrived.at[d, rows],
            send_sem=send_sem.at[c, d],
            recv_sem=recv_sem.at[c, d],
            device_id=(partners[d], v),
            device_id_type=MESH,
        )

    def small(src, dst, at, where):
        return pltpu.make_async_remote_copy(
            src_ref=src,
            dst_ref=dst,
            send_sem=small_send.at[at],
            recv_sem=small_recv.at[at],
            device_id=where,
            device_id_type=MESH,
        )

    near_copies = [
        small(min_msg, min_in.at[i], i, (near_peers[i], v)) for i in range(near - 1)
    ]
    far_copies = [
        small(min_msg2, min_in2.at[i], 7 + i, (far_peers[i], v)) for i in range(far - 1)
    ]
    x_copies = [small(old_msg, old_in.at[i], 10 + i, (s, x_peers[i])) for i in range(3)]
    z_copy = small(old_msg2, old_in2, 13, (s, z_peer))
    new_copies = [
        small(new_msg, new_in.at[i], 14 + i, (s, vel_peers[i])) for i in range(7)
    ]

    inputs = [
        pltpu.make_async_copy(src, dst, input_sem.at[i])
        for i, (src, dst) in enumerate(
            (
                (list_hbm, list_ref),
                (area_hbm, area_ref),
                (volume_hbm, volume_ref),
                (nbr_hbm, nbr_ref),
                (type_hbm, type_ref),
                (stream_hbm, stream_ref),
            )
        )
    ]
    inputs[0].start()
    load(0).start()
    for copy in inputs[1:]:
        copy.start()
    for c in range(1, CHUNKS):
        load(c).start()

    inputs[0].wait()
    send_picks[...] = one_hot(
        CELLS, 0, jnp.concatenate([list_ref[d : d + 1, :] for d in range(4)], axis=1)
    )

    def pack(c):
        rows = pl.ds(pl.multiple_of(c * CHUNK, CHUNK), CHUNK)
        high, low = two_parts(dist_v[rows, :])
        parts[c, 0:CHUNK, :] = high
        parts[c, CHUNK : 2 * CHUNK, :] = low
        both = jnp.dot(parts[c], send_picks[...], preferred_element_type=F32)
        picked = both[0:CHUNK] + both[CHUNK : 2 * CHUNK]
        for d in range(4):
            outgoing[d, rows, :] = picked[:, d * SEND : (d + 1) * SEND]

    def start_sends(c):
        for d in (2, 3, 0, 1):
            send(c, d).start()

    load(0).wait()
    pack(0)
    pl.semaphore_wait(barrier, len(greeted))
    start_sends(0)
    for copy in inputs[1:]:
        copy.wait()
    normal[...] = jnp.zeros_like(normal)
    for k in range(6):
        for axis in range(3):
            normal[axis, k : k + 1, :] = area_ref[3 * k + axis : 3 * k + axis + 1, :]
    areas = jnp.sqrt(normal[0] * normal[0] + normal[1] * normal[1] + normal[2] * normal[2])
    volume = volume_ref[...].reshape(1, CELLS)
    limit = volume / (TOP_SPEED * jnp.sum(areas, axis=0, keepdims=True))
    lowest = jnp.minimum(
        jnp.minimum(limit[:, 0:128], limit[:, 128:256]),
        jnp.minimum(limit[:, 256:384], limit[:, 384:512]),
    )
    min_msg[...] = lowest
    for copy in near_copies:
        copy.start()

    def pack_and_send(c, _):
        load(c).wait()
        pack(c)
        start_sends(c)
        return 0

    lax.fori_loop(1, FIRST, pack_and_send, 0)

    def pack_rest(c, _):
        load(c).wait()
        pack(c)
        return 0

    lax.fori_loop(FIRST, CHUNKS, pack_rest, 0)

    speed = lax.broadcasted_iota(jnp.int32, (NODES, CELLS), 0).astype(F32) - HALF
    for k in range(6):
        slope[k] = speed * normal[2, k : k + 1, :]
    for axis in range(3):
        normal[axis, 6:7, :] = jnp.sum(normal[axis, 0:6, :], axis=0, keepdims=True)
    slope[6] = speed * normal[2, 6:7, :]
    kind = type_ref[...]
    cell_ids = lax.broadcasted_iota(jnp.int32, (6, CELLS), 1)
    source[0:6, :] = jnp.where(kind == 0, nbr_ref[...], jnp.where(kind == 2, cell_ids, -1))
    inflow[0:6, :] = jnp.where(kind == 1, 1.0, 0.0)

    for i in range(14):
        start = min(i * 128, VELS - 128)
        row = stream_ref[start : start + 128].reshape(1, 128)
        stream_b[start : start + 128, :] = jnp.broadcast_to(row, (128, 128)).T

    def fill(i, _):
        k = i // 8
        base = (i % 8) * 128
        picks[k, pl.ds(pl.multiple_of(base, 128), 128), :] = one_hot(
            128, base, source[pl.ds(k, 1), :]
        )
        return 0

    lax.fori_loop(0, 48, fill, 0)

    sums[...] = jnp.zeros_like(sums)

    def old_moments(group, _):
        rows = pl.ds(pl.multiple_of(group * NODES, NODES), NODES)
        cx, cy = group_speeds(v, group)
        d = dist_v[rows, :]
        d1 = d * speed
        d2 = d1 * speed
        d3 = d2 * speed
        s0, s1, s2, s3 = fold(d), fold(d1), fold(d2), fold(d3)
        sq = cx * cx + cy * cy
        r0 = sq * s0 + s2
        terms = (
            s0,
            cx * s0,
            cy * s0,
            s1,
            (cx * cx) * s0,
            (cy * cy) * s0,
            s2,
            (cx * cy) * s0,
            cx * s1,
            cy * s1,
            cx * r0,
            cy * r0,
            sq * s1 + s3,
        )
        for i, term in enumerate(terms):
            sums[i] += term
        return 0

    lax.fori_loop(0, VELS // NODES, old_moments, 0)
    old_msg[...] = jnp.zeros_like(old_msg)
    for i in range(13):
        old_msg[i : i + 1, :] = jnp.sum(sums[i], axis=0, keepdims=True)
    for copy in near_copies:
        copy.wait()
    lowest = min_msg[...]
    for i in range(near - 1):
        lowest = jnp.minimum(lowest, min_in[i])
    min_msg2[...] = lowest
    for copy in far_copies:
        copy.start()
    for copy in x_copies:
        copy.start()

    def send_next(c, _):
        start_sends(c)
        return 0

    lax.fori_loop(FIRST, CHUNKS, send_next, 0)
    def products(lhs, first, last):
        for k in range(6):
            gathered[k] = jnp.dot(
                lhs, picks[k, first:last, :], preferred_element_type=F32
            )

    def picked_rows(k, g):
        one = pl.ds(pl.multiple_of(g * NODES, NODES), NODES)
        two = pl.ds(pl.multiple_of(CHUNK + g * NODES, NODES), NODES)
        return gathered[k, one, :] + gathered[k, two, :]

    def normal_speed(k, cx, cy):
        return (cx * normal[0, k : k + 1, :] + cy * normal[1, k : k + 1, :]) + slope[k]

    def flux(c, local, remote):
        if remote:
            arrived_rows = pl.ds(pl.multiple_of(c * CHUNK, CHUNK), CHUNK)
            for d in range(4):
                high, low = two_parts(arrived[d, arrived_rows, :])
                lanes = slice(d * SEND, (d + 1) * SEND)
                arrived_parts[0:CHUNK, lanes] = high
                arrived_parts[CHUNK : 2 * CHUNK, lanes] = low
        if local and remote:
            products(jnp.concatenate([parts[c], arrived_parts[...]], axis=1), 0, 2 * CELLS)
        elif local:
            products(parts[c], 0, CELLS)
        else:
            products(arrived_parts[...], CELLS, 2 * CELLS)

        def one_group(g, _):
            group = c * GROUPS + g
            rows = pl.ds(pl.multiple_of(group * NODES, NODES), NODES)
            cx, cy = group_speeds(v, group)
            inward = jnp.zeros((NODES, CELLS), F32)
            free = jnp.zeros((NODES, CELLS), F32)
            total = jnp.zeros((NODES, CELLS), F32)
            for k in range(6):
                u = jnp.minimum(normal_speed(k, cx, cy), 0.0)
                total += u * picked_rows(k, g)
                if local:
                    inward += u
                    free += u * inflow[k : k + 1, :]
            if local:
                stream = stream_b[rows, :]
                stream = jnp.concatenate([stream] * 4, axis=1)
                outward = normal_speed(6, cx, cy) - inward
                total += outward * dist_v[rows, :] + free * stream
            else:
                total += moved[rows, :]
            moved[rows, :] = total
            if remote:
                t1 = total * speed
                s0, s1, s2 = fold(total), fold(t1), fold(t1 * speed)
                sums[0] += s0
                sums[1] += cx * s0
                sums[2] += cy * s0
                sums[3] += s1
                sums[4] += 0.5 * ((cx * cx + cy * cy) * s0 + s2)
            return 0

        lax.fori_loop(0, GROUPS, one_group, 0, unroll=3)

    def local_part(c, _):
        flux(c, True, False)
        return 0

    lax.fori_loop(SPLIT, CHUNKS, local_part, 0)
    for i in range(5):
        sums[i] = jnp.zeros((8, CELLS), F32)

    def arrive(c):
        for d in range(4):
            send(c, d).wait_recv()

    def whole_part(c, _):
        arrive(c)

        @pl.when(c == 4)
        def _():
            for copy in x_copies:
                copy.wait()
            old_msg2[...] = old_msg[...] + old_in[0] + old_in[1] + old_in[2]
            z_copy.start()

        flux(c, True, True)
        return 0

    lax.fori_loop(0, SPLIT, whole_part, 0)

    def finish_sends(c, _):
        for d in range(4):
            send(c, d).wait_send()
        return 0

    def remote_part(c, _):
        arrive(c)
        flux(c, False, True)
        finish_sends(c - SPLIT, 0)
        return 0

    lax.fori_loop(SPLIT, CHUNKS, remote_part, 0)

    new_msg[...] = jnp.zeros_like(new_msg)
    for i in range(5):
        row = jnp.sum(sums[i], axis=0, keepdims=True)
        for t in range(4):
            new_msg[4 * i + t : 4 * i + t + 1, :] = row[:, 128 * t : 128 * t + 128]
    for copy in new_copies:
        copy.start()

    for copy in far_copies:
        copy.wait()
    lowest = min_msg2[...]
    for i in range(far - 1):
        lowest = jnp.minimum(lowest, min_in2[i])
    time_step = CFL * jnp.min(lowest, axis=1, keepdims=True)
    time_step = jnp.broadcast_to(time_step, (1, CELLS))
    z_copy.wait()
    old = old_msg2[...] + old_in2[...]
    rho = old[0:1]
    mean = [old[1 + i : 2 + i] / rho for i in range(3)]
    pressure = [[old[4:5], old[7:8], old[8:9]], [old[7:8], old[5:6], old[9:10]], [old[8:9], old[9:10], old[6:7]]]
    trace = old[4:5] + old[5:6] + old[6:7]
    mean_sq = mean[0] * mean[0] + mean[1] * mean[1] + mean[2] * mean[2]
    for i in range(3):
        along = (
            mean[0] * pressure[i][0] + mean[1] * pressure[i][1] + mean[2] * pressure[i][2]
        )
        coef_ref[8 + i : 9 + i, :] = 0.5 * (
            old[10 + i : 11 + i] - 2.0 * along - mean[i] * trace + 2.0 * rho * mean_sq * mean[i]
        )
    ratio = time_step / volume
    coef_ref[5:6, :] = ratio
    coef_ref[6:7, :] = time_step
    coef_ref[7:8, :] = jnp.zeros((1, CELLS), F32)
    coef_ref[11:16, :] = jnp.zeros((5, CELLS), F32)

    lax.fori_loop(CHUNKS - SPLIT, CHUNKS, finish_sends, 0)
    total = new_msg[...]
    for i in range(7):
        new_copies[i].wait_recv()
        total = total + new_in[i]
    for copy in new_copies:
        copy.wait_send()
    energy = 0.5 * trace
    for i in range(5):
        phi = jnp.concatenate([total[4 * i + t : 4 * i + t + 1] for t in range(4)], axis=1)
        before = energy if i == 4 else old[i : i + 1]
        coef_ref[i : i + 1, :] = before - ratio * phi


def relax(dist_v, moved, coef_ref, out_hbm, result, first, second, third, sem):
    v = lax.axis_index("vel")
    rho = coef_ref[0:1, :]
    mean = [coef_ref[1 + i : 2 + i, :] / rho for i in range(3)]
    heat = [coef_ref[8 + i : 9 + i, :] for i in range(3)]
    ratio = coef_ref[5:6, :]
    time_step = coef_ref[6:7, :]
    mean_sq = mean[0] * mean[0] + mean[1] * mean[1] + mean[2] * mean[2]
    temp = (2.0 * coef_ref[4:5, :] / rho - mean_sq) / 3.0
    relax_time = MU_REF * jnp.exp(OMEGA * jnp.log(temp)) / (rho * temp)
    relax_ratio = time_step / relax_time
    keep = 1.0 / (1.0 + relax_ratio)
    cold = 1.0 / temp
    root = lax.rsqrt(2.0 * math.pi * temp)
    scale = relax_ratio * keep * rho * (root * root * root)
    bend = (1.0 - PRANDTL) / (5.0 * rho * temp * temp)
    speed = lax.broadcasted_iota(jnp.int32, (NODES, CELLS), 0).astype(F32) - HALF
    for axis, table in ((1, second), (2, third)):
        rel = speed - mean[axis]
        sq = rel * rel * cold
        table[0] = jnp.exp(-0.5 * sq)
        table[1] = sq
        table[2] = rel * (heat[axis] * bend)
    own = lax.broadcasted_iota(jnp.int32, (8, CELLS), 0).astype(F32) - HALF
    rel = own + (v * 3).astype(F32) - mean[0]
    sq = rel * rel * cold
    first[0] = jnp.exp(-0.5 * sq) * scale
    first[1] = sq - 5.0
    first[2] = rel * (heat[0] * bend)

    def one_chunk(c, _):
        def one_group(g, _):
            group = c * GROUPS + g
            rows = pl.ds(pl.multiple_of(group * NODES, NODES), NODES)
            a = pl.ds(group // NODES, 1)
            b = pl.ds(group % NODES, 1)
            weight = first[0, a, :] * second[0, b, :]
            sq = (first[1, a, :] + second[1, b, :]) + third[1]
            along = (first[2, a, :] + second[2, b, :]) + third[2]
            gauss = weight * third[0]
            rest = dist_v[rows, :] - ratio * moved[rows, :]
            result[rows, :] = rest * keep + gauss * (1.0 + along * sq)
            return 0

        lax.fori_loop(0, GROUPS, one_group, 0, unroll=True)
        rows = pl.ds(pl.multiple_of(c * CHUNK, CHUNK), CHUNK)
        pltpu.make_async_copy(result.at[rows], out_hbm.at[rows], sem.at[c]).start()
        return 0

    lax.fori_loop(0, CHUNKS, one_chunk, 0)

    def finish(c, _):
        rows = pl.ds(pl.multiple_of(c * CHUNK, CHUNK), CHUNK)
        pltpu.make_async_copy(result.at[rows], out_hbm.at[rows], sem.at[c]).wait()
        return 0

    lax.fori_loop(0, CHUNKS, finish, 0)


def solution(mesh):
    n_space = mesh.shape["space"]
    vmem = pl.BlockSpec(memory_space=pltpu.VMEM)
    hbm = pl.BlockSpec(memory_space=pl.ANY)
    raw = pl.BlockSpec(memory_space=pltpu.HBM)

    def local(dist, free_stream, area_normal, cell_volume, face_nbr, face_type, send_list):
        own, moved, coef = pl.pallas_call(
            functools.partial(transport, n_space),
            out_shape=(
                jax.ShapeDtypeStruct((VELS, CELLS), F32),
                jax.ShapeDtypeStruct((VELS, CELLS), F32),
                jax.ShapeDtypeStruct((16, CELLS), F32),
            ),
            in_specs=[raw] * 7,
            out_specs=(vmem, vmem, vmem),
            scratch_shapes=[
                pltpu.VMEM((VELS,), F32),
                pltpu.VMEM((18, CELLS), F32),
                pltpu.VMEM((CELLS,), F32),
                pltpu.VMEM((6, CELLS), jnp.int32),
                pltpu.VMEM((6, CELLS), jnp.int32),
                pltpu.VMEM((4, SEND), jnp.int32),
                pltpu.VMEM((CHUNKS, 2 * CHUNK, CELLS), BF16),
                pltpu.VMEM((4, VELS, SEND), F32),
                pltpu.VMEM((4, VELS, SEND), F32),
                pltpu.VMEM((6, 2 * CELLS, CELLS), BF16),
                pltpu.VMEM((CELLS, CELLS), BF16),
                pltpu.VMEM((6, 2 * CHUNK, CELLS), F32),
                pltpu.VMEM((2 * CHUNK, CELLS), BF16),
                pltpu.VMEM((3, 8, CELLS), F32),
                pltpu.VMEM((7, NODES, CELLS), F32),
                pltpu.VMEM((8, CELLS), F32),
                pltpu.VMEM((8, CELLS), jnp.int32),
                pltpu.VMEM((VELS, 128), F32),
                pltpu.VMEM((13, 8, CELLS), F32),
                pltpu.VMEM((16, CELLS), F32),
                pltpu.VMEM((3, 16, CELLS), F32),
                pltpu.VMEM((16, CELLS), F32),
                pltpu.VMEM((16, CELLS), F32),
                pltpu.VMEM((24, 128), F32),
                pltpu.VMEM((7, 24, 128), F32),
                pltpu.VMEM((1, 128), F32),
                pltpu.VMEM((7, 1, 128), F32),
                pltpu.VMEM((1, 128), F32),
                pltpu.VMEM((n_space // 8 - 1, 1, 128), F32),
                pltpu.SemaphoreType.DMA((CHUNKS,)),
                pltpu.SemaphoreType.DMA((6,)),
                pltpu.SemaphoreType.DMA((CHUNKS, 4)),
                pltpu.SemaphoreType.DMA((CHUNKS, 4)),
                pltpu.SemaphoreType.DMA((21,)),
                pltpu.SemaphoreType.DMA((21,)),
            ],
            compiler_params=pltpu.CompilerParams(
                collective_id=0, has_side_effects=True, vmem_limit_bytes=44 * 2**20
            ),
            name="transport",
        )(
            *[
                pltpu.with_memory_space_constraint(x, pltpu.HBM)
                for x in (
                    dist,
                    free_stream,
                    area_normal,
                    cell_volume,
                    face_nbr,
                    face_type,
                    send_list,
                )
            ]
        )
        return pl.pallas_call(
            relax,
            out_shape=jax.ShapeDtypeStruct((VELS, CELLS), F32),
            in_specs=[vmem] * 3,
            out_specs=hbm,
            scratch_shapes=[
                pltpu.VMEM((VELS, CELLS), F32),
                pltpu.VMEM((3, 8, CELLS), F32),
                pltpu.VMEM((3, NODES, CELLS), F32),
                pltpu.VMEM((3, NODES, CELLS), F32),
                pltpu.SemaphoreType.DMA((CHUNKS,)),
            ],
            compiler_params=pltpu.CompilerParams(vmem_limit_bytes=24 * 2**20),
            name="relax",
        )(own, moved, coef)

    return jax.shard_map(
        local,
        mesh=mesh,
        in_specs=(
            P("vel", "space"),
            P("vel"),
            P(None, "space"),
            P("space"),
            P(None, "space"),
            P(None, "space"),
            P(None, "space"),
        ),
        out_specs=P("vel", "space"),
        check_vma=False,
    )
```
